128 devices in a mesh: dp: 128 (over y, z, x, core).
Axes of the slice: x: 4, y: 4, z: 4, core: 2. Of those that a mesh axis runs over, the one named last changes fastest.
Arguments:
- params: float32 [16252928], P('dp'), may hold values from -6 to 6
- first_moment: float32 [16252928], P('dp'), may hold values from -2 to 2
- second_moment: float32 [16252928], P('dp'), may hold values from 0.01 to 1
- grads: bfloat16 [16252928], P('dp'), may hold values from -6 to 6
- old_bounds: int32 [129], replicated, may hold values from 0 to 15728640, as said below
- new_bounds: int32 [129], replicated, may hold values from 0 to 15728640, as said below
- seg_start: int32 [64], replicated, may hold values from 0 to 15728576, as said below
Outputs:
- new_params: float32 [16252928], P('dp')
- new_first: float32 [16252928], P('dp')
- new_second: float32 [16252928], P('dp')
The draws below stay inside these ranges and needn't reach their ends.
Inputs may be any that keep to these rules, and one draw needn't show every extreme that they name: `old_bounds`: starts at 0 and ends at 15728640; every shard holds between 118784 and 126976 elements, exactly 126976 in some shard. `new_bounds`: starts at 0 and ends at 15728640; every shard holds between 118784 and 126976 elements, exactly 126976 in some shard; each entry differs from the same entry of old_bounds by at most 4096, by exactly 4096 somewhere. `seg_start`: strictly rising, the first is 0, all are multiples of 64.
All inputs are finite; a program needn't handle non-finite values.
Results may differ from the reference program's by a relative error of at most 0.0003.
Values sent between devices are 32-bit elements; how exact they have to be, the bound alone decides.
No kernel may reach another device: no remote copies, remote signals or barrier semaphores. Data moves between devices by JAX's collectives and lax.ppermute only.
A program may use at most 64 MiB of HBM per device.

```python
import math
import jax
import jax.numpy as jnp

BASE = 122880
MARGIN = 4096
SEGS = 64
CAP = 126976
TOTAL = 15728640
N_DP = 128


def bounds_pair(key):
    half = MARGIN // 2
    first = jax.random.randint(jax.random.fold_in(key, 11), (N_DP + 1,), -half, half + 1)
    second = jax.random.randint(jax.random.fold_in(key, 12), (N_DP + 1,), -half, half + 1)
    where_at = jax.random.randint(jax.random.fold_in(key, 13), (), 1, N_DP - 2)
    index = jnp.arange(N_DP + 1, dtype=jnp.int32)
    first = jnp.where(index == where_at, -half, first)
    first = jnp.where(index == where_at + 1, half, first)
    second = jnp.where(index == where_at + 1, -half, second)
    second = jnp.where(index == where_at + 2, half, second)
    edges = (index == 0) | (index == N_DP)
    first = jnp.where(edges, 0, first)
    second = jnp.where(edges, 0, second)
    nominal = index * BASE
    return ((nominal + first).astype(jnp.int32), (nominal + second).astype(jnp.int32))


def draw_old_bounds(key, part):
    return bounds_pair(key)[0]


def draw_new_bounds(key, part):
    return bounds_pair(key)[1]


def draw_seg_start(key, part):
    picks = jax.random.permutation(jax.random.fold_in(key, 21), TOTAL // 64 - 1)[:SEGS - 1] + 1
    picks = jnp.sort(picks.astype(jnp.int32))
    return jnp.concatenate([jnp.zeros((1,), jnp.int32), picks * 64]).astype(jnp.int32)


def level_of(rng, dims, cuts, least, largest):
    loudness = 1.0
    for dim, blocks in cuts:
        heights = jax.random.uniform(jax.random.fold_in(jax.random.fold_in(rng, 6), dim), (blocks,), jnp.float32, least / len(cuts), largest / len(cuts))
        loudness = loudness * jnp.repeat(jnp.exp(heights), dims[dim] // blocks).reshape((-1,) + (1,) * (len(dims) - 1 - dim))
    return loudness


def normal_values(key, extent, spread, bound, pieces=(), kind=jnp.bfloat16):
    level = level_of(key, extent, pieces, -0.22, 0.18) if pieces else 1.0
    result = jax.random.normal(key, extent, jnp.float32) * spread * level
    return jnp.minimum(jnp.maximum(result, -bound), bound).astype(kind)


def setup_inputs(seed: int = 0) -> dict:
    streams_of = jax.random.split(jax.random.key(seed), 8)
    params = normal_values(streams_of[0], (N_DP * CAP,), 1.0, 6.0, ((0, 128),), jnp.float32)
    first_moment = normal_values(streams_of[1], (N_DP * CAP,), 0.3, 2.0, ((0, 128),), jnp.float32)
    second_moment = jnp.clip(jnp.exp(math.log(1.0) - 4.6051702 * jax.random.uniform(streams_of[2], (N_DP * CAP,), jnp.float32) ** level_of(streams_of[2], (N_DP * CAP,), ((0, 128),), -0.2, 0.2)), 0.01, 1.0)
    grads = normal_values(streams_of[3], (N_DP * CAP,), 1.0, 6.0, ((0, 128),))
    old_bounds = draw_old_bounds(jax.random.fold_in(streams_of[7], 71), 0)
    new_bounds = draw_new_bounds(jax.random.fold_in(streams_of[7], 71), 0)
    seg_start = draw_seg_start(jax.random.fold_in(streams_of[7], 71), 0)
    return {"params": params, "first_moment": first_moment, "second_moment": second_moment, "grads": grads, "old_bounds": old_bounds, "new_bounds": new_bounds, "seg_start": seg_start}


BETA_ONE = 0.9
BETA_TWO = 0.999
CORR_ONE = 1.0 - 0.9 ** 10
CORR_TWO = 1.0 - 0.999 ** 10
DECAY = 0.01
LEARN = 0.1
EPSILON = 1e-06

def reference(params, first_moment, second_moment, grads, old_bounds, new_bounds, seg_start):
    count = N_DP
    cap = BASE + MARGIN
    total = BASE * N_DP
    position = jnp.arange(total, dtype=jnp.int32)
    owner = (jnp.searchsorted(old_bounds, position, side='right') - 1).astype(jnp.int32)
    owner = jnp.clip(owner, 0, count - 1).astype(jnp.int32)
    source = (owner * cap + (position - old_bounds[owner])).astype(jnp.int32)
    weight = params[source]
    moment = first_moment[source]
    second = second_moment[source]
    gradient = grads[source].astype(jnp.float32)
    moment_new = BETA_ONE * moment + (1.0 - BETA_ONE) * gradient
    second_new = BETA_TWO * second + (1.0 - BETA_TWO) * gradient * gradient
    update = moment_new / CORR_ONE / (jnp.sqrt(second_new / CORR_TWO) + EPSILON) + DECAY * weight
    segment = (jnp.searchsorted(seg_start, position, side='right') - 1).astype(jnp.int32)
    weight_sq = jax.ops.segment_sum(weight * weight, segment, num_segments=SEGS)
    update_sq = jax.ops.segment_sum(update * update, segment, num_segments=SEGS)
    ratio = jnp.sqrt(weight_sq) / (jnp.sqrt(update_sq) + EPSILON)
    weight_new = weight - LEARN * ratio[segment] * update
    slot_index = jnp.arange(count * cap, dtype=jnp.int32)
    device = (slot_index // cap).astype(jnp.int32)
    within = (slot_index % cap).astype(jnp.int32)
    valid = within < new_bounds[device + 1] - new_bounds[device]
    target = jnp.clip(new_bounds[device] + within, 0, total - 1).astype(jnp.int32)
    zero = jnp.float32(0.0)
    return (jnp.where(valid, weight_new[target], zero), jnp.where(valid, moment_new[target], zero), jnp.where(valid, second_new[target], zero))
```

```python
import jax
import jax.numpy as jnp
from jax import lax
from jax.experimental import pallas as pl
from jax.experimental.pallas import tpu as pltpu
from jax.sharding import PartitionSpec as P

MARGIN = 4096
SEGS = 64
N_DP = 128
LANES = 128
ROWS = 992
RIM = MARGIN // LANES
PAD_ROWS = 1032

BETA_ONE = 0.9
BETA_TWO = 0.999
CORR_ONE = 1.0 - 0.9**10
CORR_TWO = 1.0 - 0.999**10
DECAY = 0.01
LEARN = 0.1
EPSILON = 1e-06

BLOCK = 32
BLOCK_ELEMS = BLOCK * LANES


def lanes_of(rows):
    return lax.broadcasted_iota(jnp.int32, (rows, LANES), 1)


def index_of(rows):
    return lax.broadcasted_iota(jnp.int32, (rows, LANES), 0) * LANES + lanes_of(rows)


def segment_range(seg, low, high):
    first = jnp.int32(-1)
    last = jnp.int32(-1)
    for s in range(SEGS):
        start = seg[s]
        first = first + jnp.where(start <= low, 1, 0)
        last = last + jnp.where(start < high, 1, 0)
    return first, last


def segment_span(seg, s, low, high):
    begin = jnp.maximum(seg[s], low) - low
    following = jnp.where(s == SEGS - 1, high, seg[jnp.minimum(s + 1, SEGS - 1)])
    end = jnp.minimum(following, high) - low
    return begin, end


def prepare(w_hbm, m_hbm, v_hbm, g_hbm, old, seg, pay, w_own, m_own, v_own, u_own, send_core, send_next, m_in, v_in, g_in, sems):
    copies = [
        pltpu.make_async_copy(w_hbm, w_own.at[pl.ds(0, ROWS)], sems.at[0]),
        pltpu.make_async_copy(m_hbm, m_in, sems.at[1]),
        pltpu.make_async_copy(v_hbm, v_in, sems.at[2]),
        pltpu.make_async_copy(g_hbm, g_in, sems.at[3]),
    ]
    for copy in copies:
        copy.start()
    device = lax.axis_index("dp")
    low = old[device]
    high = old[device + 1]
    count = high - low
    first, last = segment_range(seg, low, high)
    for copy in copies:
        copy.wait()

    def update(b, carry):
        rows = pl.ds(pl.multiple_of(b * BLOCK, BLOCK), BLOCK)
        grad = g_in[rows, :].astype(jnp.float32)
        weight = w_own[rows, :]
        moment = BETA_ONE * m_in[rows, :] + (1.0 - BETA_ONE) * grad
        second = BETA_TWO * v_in[rows, :] + (1.0 - BETA_TWO) * grad * grad
        step = moment / CORR_ONE / (jnp.sqrt(second / CORR_TWO) + EPSILON) + DECAY * weight
        m_own[rows, :] = moment
        v_own[rows, :] = second
        u_own[rows, :] = step
        return carry

    lax.fori_loop(0, ROWS // BLOCK, update, 0)

    cut = count - MARGIN
    cut_row = cut // LANES
    cut_lane = lax.rem(cut, LANES)
    back = lax.rem(LANES - cut_lane, LANES)
    even = lax.rem(device, 2) == 0

    def write_rims(head, tail):
        for a, source in enumerate((w_own, m_own, v_own, u_own)):
            head[a] = source[pl.ds(0, RIM), :]
            here = source[pl.ds(cut_row, RIM), :]
            below = source[pl.ds(cut_row + 1, RIM), :]
            tail[a] = pltpu.roll(jnp.where(lanes_of(RIM) >= cut_lane, here, below), back, 1)

    @pl.when(even)
    def _():
        write_rims(send_next, send_core)

    @pl.when(jnp.logical_not(even))
    def _():
        write_rims(send_core, send_next)

    element = index_of(BLOCK)
    lane = lanes_of(8)

    def fold(x):
        return x[0:8] + x[8:16] + x[16:24] + x[24:32]

    def segment(s, packed):
        begin, end = segment_span(seg, s, low, high)

        def add(b, sums):
            weight_sum, update_sum = sums
            rows = pl.ds(pl.multiple_of(b * BLOCK, BLOCK), BLOCK)
            place = element + b * BLOCK_ELEMS
            inside = (place >= begin) & (place < end)
            weight = w_own[rows, :]
            step = u_own[rows, :]
            weight_sum = weight_sum + fold(jnp.where(inside, weight * weight, 0.0))
            update_sum = update_sum + fold(jnp.where(inside, step * step, 0.0))
            return weight_sum, update_sum

        zero = jnp.zeros((8, LANES), jnp.float32)
        weight_sum, update_sum = lax.fori_loop(
            begin // BLOCK_ELEMS, (end + BLOCK_ELEMS - 1) // BLOCK_ELEMS, add, (zero, zero)
        )
        weight_sum = jnp.sum(weight_sum)
        update_sum = jnp.sum(update_sum)
        return packed + jnp.where(lane == s, weight_sum, 0.0) + jnp.where(lane == SEGS + s, update_sum, 0.0)

    packed = lax.fori_loop(first, last + 1, segment, jnp.zeros((8, LANES), jnp.float32))
    for row in range(0, N_DP, 8):
        pay[pl.ds(row, 8), :] = packed


def finish(parts, w_own, m_own, v_own, u_own, from_core, from_next, old, new, seg, w_out, m_out, v_out,
           w_new, m_new, v_new, u_new, heads, rims, sems):
    device = lax.axis_index("dp")
    old_low = old[device]
    old_high = old[device + 1]
    low = new[device]
    high = new[device + 1]
    count = high - low
    shift = low - old_low + MARGIN
    shift_row = shift // LANES
    shift_lane = lax.rem(shift, LANES)
    back = lax.rem(LANES - shift_lane, LANES)
    even = lax.rem(device, 2) == 0
    owns = (w_own, m_own, v_own, u_own)
    news = (w_new, m_new, v_new, u_new)

    def split_rims(left, right):
        for a in range(4):
            heads[a, pl.ds(0, RIM), :] = left[a]
            rims[a, pl.ds(8, RIM), :] = right[a]

    @pl.when(even)
    def _():
        split_rims(from_next, from_core)

    @pl.when(jnp.logical_not(even))
    def _():
        split_rims(from_core, from_next)

    for a in range(4):
        heads[a, pl.ds(RIM, 72), :] = owns[a][pl.ds(0, 72), :]

    element = index_of(BLOCK)
    keep = lanes_of(BLOCK) >= shift_lane

    def moved(here, below, live):
        return jnp.where(live, pltpu.roll(jnp.where(keep, here, below), back, 1), 0.0)

    for a in range(4):
        here = heads[a, pl.ds(shift_row, BLOCK), :]
        below = heads[a, pl.ds(shift_row + 1, BLOCK), :]
        news[a][pl.ds(0, BLOCK), :] = moved(here, below, element < count)

    def move(b, carry):
        live = element + b * BLOCK_ELEMS < count
        source = b * BLOCK + shift_row - RIM
        rows = pl.ds(pl.multiple_of(b * BLOCK, BLOCK), BLOCK)
        for a in range(4):
            here = owns[a][pl.ds(source, BLOCK), :]
            below = owns[a][pl.ds(source + 1, BLOCK), :]
            news[a][rows, :] = moved(here, below, live)
        return carry

    lax.fori_loop(1, ROWS // BLOCK, move, 0)

    cut = old_high - low

    @pl.when(cut < count)
    def _():
        cut_row = cut // LANES
        cut_lane = lax.rem(cut, LANES)
        place = index_of(40) + cut_row * LANES
        taken = (place >= cut) & (place < count)
        fits = lanes_of(40) < LANES - cut_lane
        for a in range(4):
            here = rims[a, pl.ds(8, 40), :]
            above = rims[a, pl.ds(7, 40), :]
            incoming = pltpu.roll(jnp.where(fits, here, above), cut_lane, 1)
            rows = pl.ds(cut_row, 40)
            news[a][rows, :] = jnp.where(taken, incoming, news[a][rows, :])

    m_copy = pltpu.make_async_copy(m_new.at[pl.ds(0, ROWS)], m_out, sems.at[0])
    v_copy = pltpu.make_async_copy(v_new.at[pl.ds(0, ROWS)], v_out, sems.at[1])
    m_copy.start()
    v_copy.start()

    sums = jnp.broadcast_to(jnp.sum(parts[...], axis=0, keepdims=True), (8, LANES))
    ratio = jnp.sqrt(sums) / (jnp.sqrt(pltpu.roll(sums, SEGS, 1)) + EPSILON)
    lane = lanes_of(8)
    first, last = segment_range(seg, low, high)

    def segment(s, carry):
        begin, end = segment_span(seg, s, low, high)
        rate = LEARN * jnp.sum(jnp.where(lane == s, ratio, 0.0), axis=1, keepdims=True)[0:1]

        def apply(b, inner):
            rows = pl.ds(pl.multiple_of(b * BLOCK, BLOCK), BLOCK)
            place = element + b * BLOCK_ELEMS
            inside = (place >= begin) & (place < end)
            weight = w_new[rows, :]
            w_new[rows, :] = jnp.where(inside, weight - rate * u_new[rows, :], weight)
            return inner

        lax.fori_loop(begin // BLOCK_ELEMS, (end + BLOCK_ELEMS - 1) // BLOCK_ELEMS, apply, 0)
        return carry

    lax.fori_loop(first, last + 1, segment, 0)
    w_copy = pltpu.make_async_copy(w_new.at[pl.ds(0, ROWS)], w_out, sems.at[2])
    w_copy.start()
    m_copy.wait()
    v_copy.wait()
    w_copy.wait()


def shards(params, first_moment, second_moment, grads, old_bounds, new_bounds, seg_start):
    any_space = pl.BlockSpec(memory_space=pl.ANY)
    vmem = pl.BlockSpec(memory_space=pltpu.VMEM)
    smem = pl.BlockSpec(memory_space=pltpu.SMEM)
    f32 = jnp.float32
    own = jax.ShapeDtypeStruct((PAD_ROWS, LANES), f32)
    rim = jax.ShapeDtypeStruct((4, RIM, LANES), f32)
    state = pltpu.VMEM((ROWS, LANES), f32)
    flat = [x.reshape(ROWS, LANES) for x in (params, first_moment, second_moment, grads)]
    pay, w_own, m_own, v_own, u_own, send_core, send_next = pl.pallas_call(
        prepare,
        out_shape=(jax.ShapeDtypeStruct((N_DP, LANES), f32), own, own, own, own, rim, rim),
        in_specs=[any_space] * 4 + [smem] * 2,
        out_specs=[vmem] * 7,
        scratch_shapes=[state, state, pltpu.VMEM((ROWS, LANES), jnp.bfloat16), pltpu.SemaphoreType.DMA((4,))],
        compiler_params=pltpu.CompilerParams(vmem_limit_bytes=24 * 2**20),
    )(*flat, old_bounds, seg_start)
    pairs = [(i, i ^ 1) for i in range(N_DP)]
    between = [(i, i + 1) for i in range(1, N_DP - 1, 2)]
    between = between + [(j, i) for i, j in between]
    from_core = lax.ppermute(send_core, "dp", pairs)
    from_next = lax.ppermute(send_next, "dp", between)
    parts = lax.all_to_all(pay, "dp", 0, 0, tiled=True)
    padded = pltpu.VMEM((PAD_ROWS, LANES), f32)
    outs = pl.pallas_call(
        finish,
        out_shape=(jax.ShapeDtypeStruct((ROWS, LANES), f32),) * 3,
        in_specs=[vmem] * 7 + [smem] * 3,
        out_specs=[any_space] * 3,
        scratch_shapes=[padded] * 4
        + [pltpu.VMEM((4, 104, LANES), f32), pltpu.VMEM((4, 48, LANES), f32), pltpu.SemaphoreType.DMA((3,))],
        compiler_params=pltpu.CompilerParams(vmem_limit_bytes=24 * 2**20),
    )(parts, w_own, m_own, v_own, u_own, from_core, from_next, old_bounds, new_bounds, seg_start)
    return tuple(x.reshape(-1) for x in outs)


def solution(mesh):
    return jax.shard_map(
        shards,
        mesh=mesh,
        in_specs=(P("dp"), P("dp"), P("dp"), P("dp"), P(), P(), P()),
        out_specs=(P("dp"), P("dp"), P("dp")),
        check_vma=False,
    )
```

```python
import jax
import jax.numpy as jnp
from jax import lax
from jax.experimental import pallas as pl
from jax.experimental.pallas import tpu as pltpu
from jax.sharding import PartitionSpec as P

MARGIN = 4096
SEGS = 64
N_DP = 128
LANES = 128
ROWS = 992
RIM = MARGIN // LANES
PAD_ROWS = 1032

BETA_ONE = 0.9
BETA_TWO = 0.999
CORR_ONE = 1.0 - 0.9**10
CORR_TWO = 1.0 - 0.999**10
DECAY = 0.01
LEARN = 0.1
EPSILON = 1e-06

BLOCK = 32
BLOCK_ELEMS = BLOCK * LANES
BLOCKS = ROWS // BLOCK
PIECES = ((0, 8), (8, 16), (16, 24), (24, 31))


def lanes_of(rows):
    return lax.broadcasted_iota(jnp.int32, (rows, LANES), 1)


def index_of(rows):
    return lax.broadcasted_iota(jnp.int32, (rows, LANES), 0) * LANES + lanes_of(rows)


def segment_range(seg, low, high):
    first = jnp.int32(-1)
    last = jnp.int32(-1)
    for s in range(SEGS):
        start = seg[s]
        first = first + jnp.where(start <= low, 1, 0)
        last = last + jnp.where(start < high, 1, 0)
    return first, last


def segment_span(seg, s, low, high):
    begin = jnp.maximum(seg[s], low) - low
    following = jnp.where(s == SEGS - 1, high, seg[jnp.minimum(s + 1, SEGS - 1)])
    end = jnp.minimum(following, high) - low
    return begin, end


def fold(x):
    return x[0:8] + x[8:16] + x[16:24] + x[24:32]


def prepare(w_hbm, m_hbm, v_hbm, g_hbm, old_hbm, seg_hbm, pay, w_own, m_own, v_own, u_own, send_core, send_next,
            m_in, v_in, g_in, weight_sums, update_sums, old, seg, sems, scalar_sems):
    scalar_copies = [
        pltpu.make_async_copy(old_hbm, old, scalar_sems.at[0]),
        pltpu.make_async_copy(seg_hbm, seg, scalar_sems.at[1]),
    ]
    for copy in scalar_copies:
        copy.start()
    pieces = []
    for p, (begin, end) in enumerate(PIECES):
        rows = pl.ds(begin * BLOCK, (end - begin) * BLOCK)
        pieces.append([
            pltpu.make_async_copy(source.at[rows], target.at[rows], sems.at[p, a])
            for a, (source, target) in enumerate(((g_hbm, g_in), (v_hbm, v_in), (m_hbm, m_in), (w_hbm, w_own)))
        ])
        for copy in pieces[-1]:
            copy.start()
    device = lax.axis_index("dp")
    for copy in scalar_copies:
        copy.wait()
    low = old[device]
    high = old[device + 1]
    count = high - low
    first, last = segment_range(seg, low, high)

    def update(b, carry):
        rows = pl.ds(pl.multiple_of(b * BLOCK, BLOCK), BLOCK)
        grad = g_in[rows, :].astype(jnp.float32)
        weight = w_own[rows, :]
        moment = BETA_ONE * m_in[rows, :] + (1.0 - BETA_ONE) * grad
        second = BETA_TWO * v_in[rows, :] + (1.0 - BETA_TWO) * grad * grad
        step = moment * (1.0 / CORR_ONE) / (jnp.sqrt(second * (1.0 / CORR_TWO)) + EPSILON) + DECAY * weight
        m_own[rows, :] = moment
        v_own[rows, :] = second
        u_own[rows, :] = step
        short = pl.ds(pl.multiple_of(b * 8, 8), 8)
        weight_sums[short, :] = fold(weight * weight)
        update_sums[short, :] = fold(step * step)
        return carry

    for (begin, end), copies in zip(PIECES, pieces):
        for copy in copies:
            copy.wait()
        lax.fori_loop(begin, end, update, 0, unroll=True)

    cut = count - MARGIN
    cut_row = cut // LANES
    cut_lane = lax.rem(cut, LANES)
    back = lax.rem(LANES - cut_lane, LANES)
    even = lax.rem(device, 2) == 0

    def write_rims(head, tail):
        for a, source in enumerate((w_own, m_own, v_own, u_own)):
            head[a] = source[pl.ds(0, RIM), :]
            here = source[pl.ds(cut_row, RIM), :]
            below = source[pl.ds(cut_row + 1, RIM), :]
            tail[a] = pltpu.roll(jnp.where(lanes_of(RIM) >= cut_lane, here, below), back, 1)

    @pl.when(even)
    def _():
        write_rims(send_next, send_core)

    @pl.when(jnp.logical_not(even))
    def _():
        write_rims(send_core, send_next)

    element = index_of(BLOCK)
    lane = lanes_of(8)

    def segment(s, packed):
        begin, end = segment_span(seg, s, low, high)
        first_block = begin // BLOCK_ELEMS
        last_block = (end - 1) // BLOCK_ELEMS

        def edge(b, sums):
            weight_sum, update_sum = sums
            rows = pl.ds(pl.multiple_of(b * BLOCK, BLOCK), BLOCK)
            place = element + b * BLOCK_ELEMS
            inside = (place >= begin) & (place < end)
            weight = w_own[rows, :]
            step = u_own[rows, :]
            weight_sum = weight_sum + fold(jnp.where(inside, weight * weight, 0.0))
            update_sum = update_sum + fold(jnp.where(inside, step * step, 0.0))
            return weight_sum, update_sum

        def whole(b, sums):
            weight_sum, update_sum = sums
            short = pl.ds(pl.multiple_of(b * 8, 8), 8)
            return weight_sum + weight_sums[short, :], update_sum + update_sums[short, :]

        zero = jnp.zeros((8, LANES), jnp.float32)
        sums = edge(first_block, (zero, zero))
        sums = lax.fori_loop(first_block + 1, last_block, whole, sums)
        weight_sum, update_sum = lax.fori_loop(jnp.maximum(last_block, first_block + 1), last_block + 1, edge, sums)
        weight_sum = jnp.sum(weight_sum)
        update_sum = jnp.sum(update_sum)
        return packed + jnp.where(lane == s, weight_sum, 0.0) + jnp.where(lane == SEGS + s, update_sum, 0.0)

    packed = lax.fori_loop(first, last + 1, segment, jnp.zeros((8, LANES), jnp.float32))
    for row in range(0, N_DP, 8):
        pay[pl.ds(row, 8), :] = packed


def finish(parts, w_own, m_own, v_own, u_own, from_core, from_next, old_hbm, new_hbm, seg_hbm, w_out, m_out, v_out,
           w_new, m_new, v_new, u_new, heads, rims, old, new, seg, sems, scalar_sems):
    scalar_copies = [
        pltpu.make_async_copy(old_hbm, old, scalar_sems.at[0]),
        pltpu.make_async_copy(new_hbm, new, scalar_sems.at[1]),
        pltpu.make_async_copy(seg_hbm, seg, scalar_sems.at[2]),
    ]
    for copy in scalar_copies:
        copy.start()
    device = lax.axis_index("dp")
    sums = jnp.broadcast_to(jnp.sum(parts[...], axis=0, keepdims=True), (8, LANES))
    ratio = jnp.sqrt(sums) / (jnp.sqrt(pltpu.roll(sums, SEGS, 1)) + EPSILON)
    for copy in scalar_copies:
        copy.wait()
    old_low = old[device]
    old_high = old[device + 1]
    low = new[device]
    high = new[device + 1]
    count = high - low
    shift = low - old_low + MARGIN
    shift_row = shift // LANES
    shift_lane = lax.rem(shift, LANES)
    back = lax.rem(LANES - shift_lane, LANES)
    even = lax.rem(device, 2) == 0
    owns = (w_own, m_own, v_own, u_own)
    news = (w_new, m_new, v_new, u_new)

    def split_rims(left, right):
        for a in range(4):
            heads[a, pl.ds(0, RIM), :] = left[a]
            rims[a, pl.ds(8, RIM), :] = right[a]

    @pl.when(even)
    def _():
        split_rims(from_next, from_core)

    @pl.when(jnp.logical_not(even))
    def _():
        split_rims(from_core, from_next)

    for a in range(4):
        heads[a, pl.ds(RIM, 72), :] = owns[a][pl.ds(0, 72), :]

    element = index_of(BLOCK)
    keep = lanes_of(BLOCK) >= shift_lane

    def moved(here, below, live):
        return jnp.where(live, pltpu.roll(jnp.where(keep, here, below), back, 1), 0.0)

    for a in range(4):
        here = heads[a, pl.ds(shift_row, BLOCK), :]
        below = heads[a, pl.ds(shift_row + 1, BLOCK), :]
        news[a][pl.ds(0, BLOCK), :] = moved(here, below, element < count)

    def move(b, carry):
        live = element + b * BLOCK_ELEMS < count
        source = b * BLOCK + shift_row - RIM
        rows = pl.ds(pl.multiple_of(b * BLOCK, BLOCK), BLOCK)
        for a in range(4):
            here = owns[a][pl.ds(source, BLOCK), :]
            below = owns[a][pl.ds(source + 1, BLOCK), :]
            news[a][rows, :] = moved(here, below, live)
        return carry

    lax.fori_loop(1, BLOCKS, move, 0, unroll=6)

    cut = old_high - low

    @pl.when(cut < count)
    def _():
        cut_row = cut // LANES
        cut_lane = lax.rem(cut, LANES)
        place = index_of(40) + cut_row * LANES
        taken = (place >= cut) & (place < count)
        fits = lanes_of(40) < LANES - cut_lane
        for a in range(4):
            here = rims[a, pl.ds(8, 40), :]
            above = rims[a, pl.ds(7, 40), :]
            incoming = pltpu.roll(jnp.where(fits, here, above), cut_lane, 1)
            rows = pl.ds(cut_row, 40)
            news[a][rows, :] = jnp.where(taken, incoming, news[a][rows, :])

    m_copy = pltpu.make_async_copy(m_new.at[pl.ds(0, ROWS)], m_out, sems.at[0])
    v_copy = pltpu.make_async_copy(v_new.at[pl.ds(0, ROWS)], v_out, sems.at[1])
    m_copy.start()
    v_copy.start()

    lane = lanes_of(8)
    first, last = segment_range(seg, low, high)

    def segment(s, carry):
        begin, end = segment_span(seg, s, low, high)
        rate = LEARN * jnp.sum(jnp.where(lane == s, ratio, 0.0), axis=1, keepdims=True)[0:1]

        def apply(b, inner):
            rows = pl.ds(pl.multiple_of(b * BLOCK, BLOCK), BLOCK)
            place = element + b * BLOCK_ELEMS
            inside = (place >= begin) & (place < end)
            weight = w_new[rows, :]
            w_new[rows, :] = jnp.where(inside, weight - rate * u_new[rows, :], weight)
            return inner

        lax.fori_loop(begin // BLOCK_ELEMS, (end + BLOCK_ELEMS - 1) // BLOCK_ELEMS, apply, 0)
        return carry

    lax.fori_loop(first, last + 1, segment, 0)
    w_copy = pltpu.make_async_copy(w_new.at[pl.ds(0, ROWS)], w_out, sems.at[2])
    w_copy.start()
    m_copy.wait()
    v_copy.wait()
    w_copy.wait()


def in_hbm(*arrays):
    return [pltpu.with_memory_space_constraint(x, pltpu.HBM) for x in arrays]


def shards(params, first_moment, second_moment, grads, old_bounds, new_bounds, seg_start):
    hbm = pl.BlockSpec(memory_space=pltpu.HBM)
    vmem = pl.BlockSpec(memory_space=pltpu.VMEM)
    bounds = pltpu.SMEM((N_DP + 1,), jnp.int32)
    starts = pltpu.SMEM((SEGS,), jnp.int32)
    block_sums = pltpu.VMEM((BLOCKS * 8, LANES), jnp.float32)
    f32 = jnp.float32
    own = jax.ShapeDtypeStruct((PAD_ROWS, LANES), f32)
    rim = jax.ShapeDtypeStruct((4, RIM, LANES), f32)
    state = pltpu.VMEM((ROWS, LANES), f32)
    flat = [x.reshape(ROWS, LANES) for x in (params, first_moment, second_moment, grads)]
    pay, w_own, m_own, v_own, u_own, send_core, send_next = pl.pallas_call(
        prepare,
        out_shape=(jax.ShapeDtypeStruct((N_DP, LANES), f32), own, own, own, own, rim, rim),
        in_specs=[hbm] * 6,
        out_specs=[vmem] * 7,
        scratch_shapes=[state, state, pltpu.VMEM((ROWS, LANES), jnp.bfloat16), block_sums, block_sums, bounds, starts,
                        pltpu.SemaphoreType.DMA((4, 4)), pltpu.SemaphoreType.DMA((2,))],
        compiler_params=pltpu.CompilerParams(vmem_limit_bytes=24 * 2**20),
    )(*in_hbm(*flat, old_bounds, seg_start))
    pairs = [(i, i ^ 1) for i in range(N_DP)]
    between = [(i, i + 1) for i in range(1, N_DP - 1, 2)]
    between = between + [(j, i) for i, j in between]
    from_core = lax.ppermute(send_core, "dp", pairs)
    from_next = lax.ppermute(send_next, "dp", between)
    parts = lax.all_to_all(pay, "dp", 0, 0, tiled=True)
    padded = pltpu.VMEM((PAD_ROWS, LANES), f32)
    outs = pl.pallas_call(
        finish,
        out_shape=(jax.ShapeDtypeStruct((ROWS, LANES), f32),) * 3,
        in_specs=[vmem] * 7 + [hbm] * 3,
        out_specs=[hbm] * 3,
        scratch_shapes=[padded] * 4
        + [pltpu.VMEM((4, 104, LANES), f32), pltpu.VMEM((4, 48, LANES), f32), bounds, bounds, starts,
           pltpu.SemaphoreType.DMA((3,)), pltpu.SemaphoreType.DMA((3,))],
        compiler_params=pltpu.CompilerParams(vmem_limit_bytes=24 * 2**20),
    )(parts, w_own, m_own, v_own, u_own, from_core, from_next, *in_hbm(old_bounds, new_bounds, seg_start))
    return tuple(x.reshape(-1) for x in outs)


def solution(mesh):
    return jax.shard_map(
        shards,
        mesh=mesh,
        in_specs=(P("dp"), P("dp"), P("dp"), P("dp"), P(), P(), P()),
        out_specs=(P("dp"), P("dp"), P("dp")),
        check_vma=False,
    )
```

```python
import jax
import jax.numpy as jnp
from jax import lax
from jax.experimental import pallas as pl
from jax.experimental.pallas import tpu as pltpu
from jax.sharding import PartitionSpec as P

MARGIN = 4096
SEGS = 64
N_DP = 128
LANES = 128
ROWS = 992
RIM = MARGIN // LANES
PAD_ROWS = 1032
TAIL = 896
TAIL_ROWS = ROWS - TAIL

BETA_ONE = 0.9
BETA_TWO = 0.999
CORR_ONE = 1.0 - 0.9**10
CORR_TWO = 1.0 - 0.999**10
DECAY = 0.01
LEARN = 0.1
EPSILON = 1e-06

BLOCK = 32
BLOCK_ELEMS = BLOCK * LANES
BLOCKS = ROWS // BLOCK
PIECES = ((0, 8), (8, 16), (16, 24), (24, 31))


def lanes_of(rows):
    return lax.broadcasted_iota(jnp.int32, (rows, LANES), 1)


def index_of(rows):
    return lax.broadcasted_iota(jnp.int32, (rows, LANES), 0) * LANES + lanes_of(rows)


def segment_range(seg, low, high):
    first = jnp.int32(-1)
    last = jnp.int32(-1)
    for s in range(SEGS):
        start = seg[s]
        first = first + jnp.where(start <= low, 1, 0)
        last = last + jnp.where(start < high, 1, 0)
    return first, last


def segment_span(seg, s, low, high):
    begin = jnp.maximum(seg[s], low) - low
    following = jnp.where(s == SEGS - 1, high, seg[jnp.minimum(s + 1, SEGS - 1)])
    end = jnp.minimum(following, high) - low
    return begin, end


def is_early(device):
    return (device // 8 % 4 + device // 32 <= 1) & (device % 8 < 4)


def move_interior(owns, news, seg_map, seg, low, high, shift):
    shift_row = shift // LANES
    shift_lane = lax.rem(shift, LANES)
    back = lax.rem(LANES - shift_lane, LANES)
    keep = lanes_of(BLOCK) >= shift_lane

    def move(b, carry):
        source = b * BLOCK + shift_row - RIM
        rows = pl.ds(pl.multiple_of(b * BLOCK, BLOCK), BLOCK)
        for own, fresh in zip(owns, news):
            here = own[pl.ds(source, BLOCK), :]
            below = own[pl.ds(source + 1, BLOCK), :]
            fresh[rows, :] = pltpu.roll(jnp.where(keep, here, below), back, 1)
        return carry

    lax.fori_loop(1, BLOCKS, move, 0, unroll=6)
    first, last = segment_range(seg, low, high)
    element = index_of(BLOCK)

    def segment(s, carry):
        begin, end = segment_span(seg, s, low, high)
        first_block = begin // BLOCK_ELEMS
        last_block = jnp.where(s == last, BLOCKS - 1, (end - 1) // BLOCK_ELEMS)
        rows = pl.ds(pl.multiple_of(first_block * BLOCK, BLOCK), BLOCK)
        seg_map[rows, :] = jnp.where(element + first_block * BLOCK_ELEMS >= begin, s, seg_map[rows, :])

        def fill(b, inner):
            seg_map[pl.ds(pl.multiple_of(b * BLOCK, BLOCK), BLOCK), :] = jnp.full((BLOCK, LANES), s, jnp.int32)
            return inner

        lax.fori_loop(first_block + 1, last_block + 1, fill, 0)
        return carry

    lax.fori_loop(first, last + 1, segment, 0)


def fold(x):
    return x[0:8] + x[8:16] + x[16:24] + x[24:32]


def prepare(w_hbm, m_hbm, v_hbm, g_hbm, old_hbm, new_hbm, seg_hbm,
            pay, w_own, m_own, v_own, u_own, send_core, send_next, w_new, m_new, v_new, u_new, seg_map,
            m_in, v_in, g_in, weight_sums, update_sums, table, old, new, seg, sems, scalar_sems):
    scalar_copies = [
        pltpu.make_async_copy(old_hbm, old, scalar_sems.at[0]),
        pltpu.make_async_copy(seg_hbm, seg, scalar_sems.at[1]),
        pltpu.make_async_copy(new_hbm, new, scalar_sems.at[2]),
    ]
    for copy in scalar_copies:
        copy.start()
    pieces = []
    for p, (begin, end) in enumerate(PIECES):
        rows = pl.ds(begin * BLOCK, (end - begin) * BLOCK)
        pieces.append([
            pltpu.make_async_copy(source.at[rows], target.at[rows], sems.at[p, a])
            for a, (source, target) in enumerate(((g_hbm, g_in), (v_hbm, v_in), (m_hbm, m_in), (w_hbm, w_own)))
        ])
        for copy in pieces[-1]:
            copy.start()
    device = lax.axis_index("dp")
    table[...] = jnp.zeros((2 * SEGS, LANES), jnp.float32)
    for copy in scalar_copies:
        copy.wait()
    low = old[device]
    high = old[device + 1]
    count = high - low
    first, last = segment_range(seg, low, high)

    def update(b, carry):
        rows = pl.ds(pl.multiple_of(b * BLOCK, BLOCK), BLOCK)
        grad = g_in[rows, :].astype(jnp.float32)
        weight = w_own[rows, :]
        moment = BETA_ONE * m_in[rows, :] + (1.0 - BETA_ONE) * grad
        second = BETA_TWO * v_in[rows, :] + (1.0 - BETA_TWO) * grad * grad
        step = moment * (1.0 / CORR_ONE) / (jnp.sqrt(second * (1.0 / CORR_TWO)) + EPSILON) + DECAY * weight
        m_own[rows, :] = moment
        v_own[rows, :] = second
        u_own[rows, :] = step
        short = pl.ds(pl.multiple_of(b * 8, 8), 8)
        weight_sums[short, :] = fold(weight * weight)
        update_sums[short, :] = fold(step * step)
        return carry

    for (begin, end), copies in zip(PIECES, pieces):
        for copy in copies:
            copy.wait()
        lax.fori_loop(begin, end, update, 0, unroll=True)

    cut = count - MARGIN
    cut_row = cut // LANES
    cut_lane = lax.rem(cut, LANES)
    back = lax.rem(LANES - cut_lane, LANES)
    even = lax.rem(device, 2) == 0

    def write_rims(head, tail):
        for a, source in enumerate((w_own, m_own, v_own, u_own)):
            head[a] = source[pl.ds(0, RIM), :]
            here = source[pl.ds(cut_row, RIM), :]
            below = source[pl.ds(cut_row + 1, RIM), :]
            tail[a] = pltpu.roll(jnp.where(lanes_of(RIM) >= cut_lane, here, below), back, 1)

    @pl.when(even)
    def _():
        write_rims(send_next, send_core)

    @pl.when(jnp.logical_not(even))
    def _():
        write_rims(send_core, send_next)

    element = index_of(BLOCK)

    def segment(s, carry):
        begin, end = segment_span(seg, s, low, high)
        first_block = begin // BLOCK_ELEMS
        last_block = (end - 1) // BLOCK_ELEMS

        def edge(b, sums):
            weight_sum, update_sum = sums
            rows = pl.ds(pl.multiple_of(b * BLOCK, BLOCK), BLOCK)
            place = element + b * BLOCK_ELEMS
            inside = (place >= begin) & (place < end)
            weight = w_own[rows, :]
            step = u_own[rows, :]
            weight_sum = weight_sum + fold(jnp.where(inside, weight * weight, 0.0))
            update_sum = update_sum + fold(jnp.where(inside, step * step, 0.0))
            return weight_sum, update_sum

        def whole(b, sums):
            weight_sum, update_sum = sums
            short = pl.ds(pl.multiple_of(b * 8, 8), 8)
            return weight_sum + weight_sums[short, :], update_sum + update_sums[short, :]

        zero = jnp.zeros((8, LANES), jnp.float32)
        sums = edge(first_block, (zero, zero))
        sums = lax.fori_loop(first_block + 1, last_block, whole, sums)
        weight_sum, update_sum = lax.fori_loop(jnp.maximum(last_block, first_block + 1), last_block + 1, edge, sums)
        table[pl.ds(s, 1), :] = jnp.sum(weight_sum, axis=0, keepdims=True)
        table[pl.ds(SEGS + s, 1), :] = jnp.sum(update_sum, axis=0, keepdims=True)
        return carry

    lax.fori_loop(first, last + 1, segment, 0)
    packed = lax.dot_general(
        jnp.ones((8, LANES), jnp.float32), table[...], (((1,), (1,)), ((), ())),
        precision=lax.Precision.HIGHEST, preferred_element_type=jnp.float32,
    )
    for row in range(0, N_DP, 8):
        pay[pl.ds(row, 8), :] = packed

    @pl.when(is_early(device))
    def _():
        new_low = new[device]
        move_interior((w_own, m_own, v_own, u_own), (w_new, m_new, v_new, u_new), seg_map, seg,
                      new_low, new[device + 1], new_low - low + MARGIN)


def finish(parts, w_own, m_own, v_own, u_own, from_next, from_core, w_pre, m_pre, v_pre, u_pre, seg_pre,
           old_hbm, new_hbm, seg_hbm, w_out, m_out, v_out,
           w_late, m_late, v_late, u_late, seg_late, w_new, heads, tails, rims, old, new, seg, sems, scalar_sems):
    scalar_copies = [
        pltpu.make_async_copy(old_hbm, old, scalar_sems.at[0]),
        pltpu.make_async_copy(new_hbm, new, scalar_sems.at[1]),
        pltpu.make_async_copy(seg_hbm, seg, scalar_sems.at[2]),
    ]
    for copy in scalar_copies:
        copy.start()
    device = lax.axis_index("dp")
    early = is_early(device)
    owns = (w_own, m_own, v_own, u_own)
    outs = (w_out, m_out, v_out)
    body = pl.ds(RIM, TAIL - RIM)

    def wait_scalars():
        for copy in scalar_copies:
            copy.wait()

    def emit(news, seg_map, ready):
        body_copies = [pltpu.make_async_copy(news[a].at[body], outs[a].at[body], sems.at[a]) for a in (1, 2)]
        for copy in body_copies:
            copy.start()
        sums = jnp.broadcast_to(jnp.sum(parts[...], axis=0, keepdims=True), (8, LANES))
        rates = LEARN * jnp.sqrt(sums) / (jnp.sqrt(pltpu.roll(sums, SEGS, 1)) + EPSILON)

        def rate_of(labels):
            pieces = [jnp.take_along_axis(rates, labels[r:r + 8], axis=1) for r in range(0, labels.shape[0], 8)]
            return jnp.concatenate(pieces, axis=0)

        def apply(b, carry):
            rows = pl.ds(pl.multiple_of(b * BLOCK, BLOCK), BLOCK)
            w_new[rows, :] = news[0][rows, :] - rate_of(seg_map[rows, :]) * news[3][rows, :]
            return carry

        lax.fori_loop(1, TAIL // BLOCK, apply, 0, unroll=9)
        body_copies.append(pltpu.make_async_copy(w_new.at[body], w_out.at[body], sems.at[0]))
        body_copies[-1].start()
        if not ready:
            wait_scalars()

        low = new[device]
        count = new[device + 1] - low
        shift = low - old[device] + MARGIN
        shift_row = shift // LANES
        shift_lane = lax.rem(shift, LANES)
        back = lax.rem(LANES - shift_lane, LANES)
        even = lax.rem(device, 2) == 0

        def split_rims(left, right):
            for a in range(4):
                heads[a, pl.ds(0, RIM), :] = left[a]
                rims[a, pl.ds(8, RIM), :] = right[a]

        @pl.when(even)
        def _():
            split_rims(from_next, from_core)

        @pl.when(jnp.logical_not(even))
        def _():
            split_rims(from_core, from_next)

        keep = lanes_of(RIM) >= shift_lane
        tail_live = index_of(TAIL_ROWS) + TAIL * LANES < count
        for a in range(4):
            heads[a, pl.ds(RIM, 72), :] = owns[a][pl.ds(0, 72), :]
            here = heads[a, pl.ds(shift_row, RIM), :]
            below = heads[a, pl.ds(shift_row + 1, RIM), :]
            heads[a, pl.ds(104, RIM), :] = pltpu.roll(jnp.where(keep, here, below), back, 1)
            tails[a, pl.ds(0, TAIL_ROWS), :] = jnp.where(tail_live, news[a][pl.ds(TAIL, TAIL_ROWS), :], 0.0)
        cut = old[device + 1] - low

        @pl.when(cut < count)
        def _():
            cut_row = cut // LANES
            cut_lane = lax.rem(cut, LANES)
            place = index_of(40) + cut_row * LANES
            taken = (place >= cut) & (place < count)
            fits = lanes_of(40) < LANES - cut_lane
            rows = pl.ds(cut_row - TAIL, 40)
            for a in range(4):
                here = rims[a, pl.ds(8, 40), :]
                above = rims[a, pl.ds(7, 40), :]
                incoming = pltpu.roll(jnp.where(fits, here, above), cut_lane, 1)
                tails[a, rows, :] = jnp.where(taken, incoming, tails[a, rows, :])

        top = pl.ds(104, RIM)
        heads[0, top, :] = heads[0, top, :] - rate_of(seg_map[pl.ds(0, RIM), :]) * heads[3, top, :]
        bottom = pl.ds(0, TAIL_ROWS)
        tails[0, bottom, :] = tails[0, bottom, :] - rate_of(seg_map[pl.ds(TAIL, TAIL_ROWS), :]) * tails[3, bottom, :]
        edge_copies = []
        for a in range(3):
            edge_copies.append(pltpu.make_async_copy(heads.at[a, top], outs[a].at[pl.ds(0, RIM)], sems.at[3 + a]))
            edge_copies.append(
                pltpu.make_async_copy(tails.at[a, bottom], outs[a].at[pl.ds(TAIL, TAIL_ROWS)], sems.at[6 + a]))
        for copy in edge_copies:
            copy.start()
        for copy in body_copies + edge_copies:
            copy.wait()

    @pl.when(early)
    def _():
        emit((w_pre, m_pre, v_pre, u_pre), seg_pre, False)

    @pl.when(jnp.logical_not(early))
    def _():
        wait_scalars()
        news = (w_late, m_late, v_late, u_late)
        low = new[device]
        move_interior(owns, news, seg_late, seg, low, new[device + 1], low - old[device] + MARGIN)
        emit(news, seg_late, True)


def in_hbm(*arrays):
    return [pltpu.with_memory_space_constraint(x, pltpu.HBM) for x in arrays]


def shards(params, first_moment, second_moment, grads, old_bounds, new_bounds, seg_start):
    hbm = pl.BlockSpec(memory_space=pltpu.HBM)
    vmem = pl.BlockSpec(memory_space=pltpu.VMEM)
    bounds = pltpu.SMEM((N_DP + 1,), jnp.int32)
    starts = pltpu.SMEM((SEGS,), jnp.int32)
    block_sums = pltpu.VMEM((BLOCKS * 8, LANES), jnp.float32)
    f32 = jnp.float32
    own = jax.ShapeDtypeStruct((PAD_ROWS, LANES), f32)
    rim = jax.ShapeDtypeStruct((4, RIM, LANES), f32)
    state = pltpu.VMEM((ROWS, LANES), f32)
    flat = [x.reshape(ROWS, LANES) for x in (params, first_moment, second_moment, grads)]
    moved = jax.ShapeDtypeStruct((ROWS, LANES), f32)
    labels = jax.ShapeDtypeStruct((ROWS, LANES), jnp.int32)
    pay, w_own, m_own, v_own, u_own, send_core, send_next, *early = pl.pallas_call(
        prepare,
        out_shape=(jax.ShapeDtypeStruct((N_DP, LANES), f32), own, own, own, own, rim, rim,
                   moved, moved, moved, moved, labels),
        in_specs=[hbm] * 7,
        out_specs=[vmem] * 12,
        scratch_shapes=[state, state, pltpu.VMEM((ROWS, LANES), jnp.bfloat16), block_sums, block_sums,
                        pltpu.VMEM((2 * SEGS, LANES), f32), bounds, bounds, starts,
                        pltpu.SemaphoreType.DMA((4, 4)), pltpu.SemaphoreType.DMA((3,))],
        compiler_params=pltpu.CompilerParams(vmem_limit_bytes=24 * 2**20),
    )(*in_hbm(*flat, old_bounds, new_bounds, seg_start))
    pairs = [(i, i ^ 1) for i in range(N_DP)]
    between = [(i, (i + (1 if i % 2 else -1)) % N_DP) for i in range(N_DP)]
    from_next = lax.ppermute(send_next, "dp", between)
    from_core = lax.ppermute(send_core, "dp", pairs)
    parts = lax.all_to_all(pay, "dp", 0, 0, tiled=True)
    outs = pl.pallas_call(
        finish,
        out_shape=(jax.ShapeDtypeStruct((ROWS, LANES), f32),) * 3,
        in_specs=[vmem] * 12 + [hbm] * 3,
        out_specs=[hbm] * 3,
        scratch_shapes=[state] * 4 + [pltpu.VMEM((ROWS, LANES), jnp.int32), state]
        + [pltpu.VMEM((4, 136, LANES), f32), pltpu.VMEM((4, 136, LANES), f32), pltpu.VMEM((4, 48, LANES), f32),
           bounds, bounds, starts, pltpu.SemaphoreType.DMA((9,)), pltpu.SemaphoreType.DMA((3,))],
        compiler_params=pltpu.CompilerParams(vmem_limit_bytes=24 * 2**20),
    )(parts, w_own, m_own, v_own, u_own, from_next, from_core, *early, *in_hbm(old_bounds, new_bounds, seg_start))
    return tuple(x.reshape(-1) for x in outs)


def solution(mesh):
    return jax.shard_map(
        shards,
        mesh=mesh,
        in_specs=(P("dp"), P("dp"), P("dp"), P("dp"), P(), P(), P()),
        out_specs=(P("dp"), P("dp"), P("dp")),
        check_vma=False,
    )
```

```python
import jax
import jax.numpy as jnp
from jax import lax
from jax.experimental import pallas as pl
from jax.experimental.pallas import tpu as pltpu
from jax.sharding import PartitionSpec as P

MARGIN = 4096
SEGS = 64
N_DP = 128
LANES = 128
ROWS = 992
RIM = MARGIN // LANES
PAD_ROWS = 1032
TAIL = 896
TAIL_ROWS = ROWS - TAIL
BODY_PIECES = ((1, 14), (14, 22), (22, 28))

BETA_ONE = 0.9
BETA_TWO = 0.999
CORR_ONE = 1.0 - 0.9**10
CORR_TWO = 1.0 - 0.999**10
DECAY = 0.01
LEARN = 0.1
EPSILON = 1e-06

BLOCK = 32
BLOCK_ELEMS = BLOCK * LANES
BLOCKS = ROWS // BLOCK
PIECES = ((0, 8), (8, 16), (16, 24), (24, 31))


def lanes_of(rows):
    return lax.broadcasted_iota(jnp.int32, (rows, LANES), 1)


def index_of(rows):
    return lax.broadcasted_iota(jnp.int32, (rows, LANES), 0) * LANES + lanes_of(rows)


def segment_range(seg, low, high):
    first = jnp.int32(-1)
    last = jnp.int32(-1)
    for s in range(SEGS):
        start = seg[s]
        first = first + jnp.where(start <= low, 1, 0)
        last = last + jnp.where(start < high, 1, 0)
    return first, last


def segment_span(seg, s, low, high):
    begin = jnp.maximum(seg[s], low) - low
    following = jnp.where(s == SEGS - 1, high, seg[jnp.minimum(s + 1, SEGS - 1)])
    end = jnp.minimum(following, high) - low
    return begin, end


def is_early(device):
    return (device // 8 % 4 + device // 32 <= 1) & (device % 8 < 4)


def move_interior(owns, news, shift):
    shift_row = shift // LANES
    shift_lane = lax.rem(shift, LANES)
    back = lax.rem(LANES - shift_lane, LANES)
    keep = lanes_of(BLOCK) >= shift_lane

    def move(b, carry):
        source = b * BLOCK + shift_row - RIM
        rows = pl.ds(pl.multiple_of(b * BLOCK, BLOCK), BLOCK)
        for own, fresh in zip(owns, news):
            here = own[pl.ds(source, BLOCK), :]
            below = own[pl.ds(source + 1, BLOCK), :]
            fresh[rows, :] = pltpu.roll(jnp.where(keep, here, below), back, 1)
        return carry

    lax.fori_loop(1, BLOCKS, move, 0, unroll=True)


def label_elements(seg_map, seg, low, high):
    first, last = segment_range(seg, low, high)
    element = index_of(BLOCK)

    def segment(s, carry):
        begin, end = segment_span(seg, s, low, high)
        first_block = begin // BLOCK_ELEMS
        last_block = jnp.where(s == last, BLOCKS - 1, (end - 1) // BLOCK_ELEMS)
        rows = pl.ds(pl.multiple_of(first_block * BLOCK, BLOCK), BLOCK)
        seg_map[rows, :] = jnp.where(element + first_block * BLOCK_ELEMS >= begin, s, seg_map[rows, :])

        def fill(b, inner):
            seg_map[pl.ds(pl.multiple_of(b * BLOCK, BLOCK), BLOCK), :] = jnp.full((BLOCK, LANES), s, jnp.int32)
            return inner

        lax.fori_loop(first_block + 1, last_block + 1, fill, 0)
        return carry

    lax.fori_loop(first, last + 1, segment, 0)


def fold(x):
    return x[0:8] + x[8:16] + x[16:24] + x[24:32]


def prepare(w_hbm, m_hbm, v_hbm, g_hbm, old_hbm, new_hbm, seg_hbm,
            pay, w_own, m_own, v_own, u_own, send_core, send_next, w_new, m_new, v_new, u_new, seg_map, info,
            m_in, v_in, g_in, weight_sums, update_sums, table, old, new, seg, sems, scalar_sems):
    scalar_copies = [
        pltpu.make_async_copy(old_hbm, old, scalar_sems.at[0]),
        pltpu.make_async_copy(seg_hbm, seg, scalar_sems.at[1]),
        pltpu.make_async_copy(new_hbm, new, scalar_sems.at[2]),
    ]
    for copy in scalar_copies:
        copy.start()
    pieces = []
    for p, (begin, end) in enumerate(PIECES):
        rows = pl.ds(begin * BLOCK, (end - begin) * BLOCK)
        pieces.append([
            pltpu.make_async_copy(source.at[rows], target.at[rows], sems.at[p, a])
            for a, (source, target) in enumerate(((g_hbm, g_in), (v_hbm, v_in), (m_hbm, m_in), (w_hbm, w_own)))
        ])
        for copy in pieces[-1]:
            copy.start()
    device = lax.axis_index("dp")
    table[...] = jnp.zeros((2 * SEGS, LANES), jnp.float32)
    for copy in scalar_copies:
        copy.wait()
    low = old[device]
    high = old[device + 1]
    count = high - low
    new_low = new[device]
    new_high = new[device + 1]
    row = lax.broadcasted_iota(jnp.int32, (8, LANES), 0)
    facts = jnp.where(row == 0, new_low - low + MARGIN, new_low)
    facts = jnp.where(row == 1, high - new_low, facts)
    info[...] = jnp.where(row == 2, new_high - new_low, facts)
    first, last = segment_range(seg, low, high)

    def update(b, carry):
        rows = pl.ds(pl.multiple_of(b * BLOCK, BLOCK), BLOCK)
        grad = g_in[rows, :].astype(jnp.float32)
        weight = w_own[rows, :]
        moment = BETA_ONE * m_in[rows, :] + (1.0 - BETA_ONE) * grad
        second = BETA_TWO * v_in[rows, :] + (1.0 - BETA_TWO) * grad * grad
        step = moment * (1.0 / CORR_ONE) / (jnp.sqrt(second * (1.0 / CORR_TWO)) + EPSILON) + DECAY * weight
        m_own[rows, :] = moment
        v_own[rows, :] = second
        u_own[rows, :] = step
        short = pl.ds(pl.multiple_of(b * 8, 8), 8)
        weight_sums[short, :] = fold(weight * weight)
        update_sums[short, :] = fold(step * step)
        return carry

    for (begin, end), copies in zip(PIECES, pieces):
        for copy in copies:
            copy.wait()
        lax.fori_loop(begin, end, update, 0, unroll=True)

    cut = count - MARGIN
    cut_row = cut // LANES
    cut_lane = lax.rem(cut, LANES)
    back = lax.rem(LANES - cut_lane, LANES)
    even = lax.rem(device, 2) == 0

    def write_rims(head, tail):
        for a, source in enumerate((w_own, m_own, v_own, u_own)):
            head[a] = source[pl.ds(0, RIM), :]
            here = source[pl.ds(cut_row, RIM), :]
            below = source[pl.ds(cut_row + 1, RIM), :]
            tail[a] = pltpu.roll(jnp.where(lanes_of(RIM) >= cut_lane, here, below), back, 1)

    @pl.when(even)
    def _():
        write_rims(send_next, send_core)

    @pl.when(jnp.logical_not(even))
    def _():
        write_rims(send_core, send_next)

    element = index_of(BLOCK)

    def segment(s, carry):
        begin, end = segment_span(seg, s, low, high)
        first_block = begin // BLOCK_ELEMS
        last_block = (end - 1) // BLOCK_ELEMS

        def edge(b, sums):
            weight_sum, update_sum = sums
            rows = pl.ds(pl.multiple_of(b * BLOCK, BLOCK), BLOCK)
            place = element + b * BLOCK_ELEMS
            inside = (place >= begin) & (place < end)
            weight = w_own[rows, :]
            step = u_own[rows, :]
            weight_sum = weight_sum + fold(jnp.where(inside, weight * weight, 0.0))
            update_sum = update_sum + fold(jnp.where(inside, step * step, 0.0))
            return weight_sum, update_sum

        def whole(b, sums):
            weight_sum, update_sum = sums
            short = pl.ds(pl.multiple_of(b * 8, 8), 8)
            return weight_sum + weight_sums[short, :], update_sum + update_sums[short, :]

        zero = jnp.zeros((8, LANES), jnp.float32)
        sums = edge(first_block, (zero, zero))
        sums = lax.fori_loop(first_block + 1, last_block, whole, sums)
        weight_sum, update_sum = lax.fori_loop(jnp.maximum(last_block, first_block + 1), last_block + 1, edge, sums)
        table[pl.ds(s, 1), :] = jnp.sum(weight_sum, axis=0, keepdims=True)
        table[pl.ds(SEGS + s, 1), :] = jnp.sum(update_sum, axis=0, keepdims=True)
        return carry

    lax.fori_loop(first, last + 1, segment, 0)
    packed = lax.dot_general(
        jnp.ones((8, LANES), jnp.float32), table[...], (((1,), (1,)), ((), ())),
        precision=lax.Precision.HIGHEST, preferred_element_type=jnp.float32,
    )
    for row in range(0, N_DP, 8):
        pay[pl.ds(row, 8), :] = packed

    @pl.when(is_early(device))
    def _():
        move_interior((w_own, m_own, v_own, u_own), (w_new, m_new, v_new, u_new), new_low - low + MARGIN)
        label_elements(seg_map, seg, new_low, new_high)


def finish(parts, w_own, m_own, v_own, u_own, from_next, from_core, w_pre, m_pre, v_pre, u_pre, seg_pre,
           info, seg_hbm, w_out, m_out, v_out,
           w_late, m_late, v_late, u_late, seg_late, w_new, heads, tails, rims, seg, sems, seg_sem):
    device = lax.axis_index("dp")
    facts = info[...]
    shift = facts[0, 0]
    cut = facts[1, 0]
    count = facts[2, 0]
    low = facts[3, 0]
    early = is_early(device)
    owns = (w_own, m_own, v_own, u_own)
    outs = (w_out, m_out, v_out)
    body = pl.ds(RIM, TAIL - RIM)

    def emit(news, seg_map):
        body_copies = [pltpu.make_async_copy(news[a].at[body], outs[a].at[body], sems.at[a]) for a in (1, 2)]
        for copy in body_copies:
            copy.start()
        sums = jnp.broadcast_to(jnp.sum(parts[...], axis=0, keepdims=True), (8, LANES))
        rates = LEARN * jnp.sqrt(sums) / (jnp.sqrt(pltpu.roll(sums, SEGS, 1)) + EPSILON)

        def rate_of(labels):
            pieces = [jnp.take_along_axis(rates, labels[r:r + 8], axis=1) for r in range(0, labels.shape[0], 8)]
            return jnp.concatenate(pieces, axis=0)

        shift_row = shift // LANES
        shift_lane = lax.rem(shift, LANES)
        back = lax.rem(LANES - shift_lane, LANES)
        even = lax.rem(device, 2) == 0

        def split_rims(left, right):
            for a in range(4):
                heads[a, pl.ds(0, RIM), :] = left[a]
                rims[a, pl.ds(8, RIM), :] = right[a]

        @pl.when(even)
        def _():
            split_rims(from_next, from_core)

        @pl.when(jnp.logical_not(even))
        def _():
            split_rims(from_core, from_next)

        keep = lanes_of(RIM) >= shift_lane
        tail_live = index_of(TAIL_ROWS) + TAIL * LANES < count
        for a in range(4):
            heads[a, pl.ds(RIM, 72), :] = owns[a][pl.ds(0, 72), :]
            here = heads[a, pl.ds(shift_row, RIM), :]
            below = heads[a, pl.ds(shift_row + 1, RIM), :]
            heads[a, pl.ds(104, RIM), :] = pltpu.roll(jnp.where(keep, here, below), back, 1)
            tails[a, pl.ds(0, TAIL_ROWS), :] = jnp.where(tail_live, news[a][pl.ds(TAIL, TAIL_ROWS), :], 0.0)

        @pl.when(cut < count)
        def _():
            cut_row = cut // LANES
            cut_lane = lax.rem(cut, LANES)
            place = index_of(40) + cut_row * LANES
            taken = (place >= cut) & (place < count)
            fits = lanes_of(40) < LANES - cut_lane
            rows = pl.ds(cut_row - TAIL, 40)
            for a in range(4):
                here = rims[a, pl.ds(8, 40), :]
                above = rims[a, pl.ds(7, 40), :]
                incoming = pltpu.roll(jnp.where(fits, here, above), cut_lane, 1)
                tails[a, rows, :] = jnp.where(taken, incoming, tails[a, rows, :])

        top = pl.ds(104, RIM)
        heads[0, top, :] = heads[0, top, :] - rate_of(seg_map[pl.ds(0, RIM), :]) * heads[3, top, :]
        bottom = pl.ds(0, TAIL_ROWS)
        tails[0, bottom, :] = tails[0, bottom, :] - rate_of(seg_map[pl.ds(TAIL, TAIL_ROWS), :]) * tails[3, bottom, :]
        edge_copies = []
        for a in range(3):
            edge_copies.append(pltpu.make_async_copy(heads.at[a, top], outs[a].at[pl.ds(0, RIM)], sems.at[3 + a]))
            edge_copies.append(
                pltpu.make_async_copy(tails.at[a, bottom], outs[a].at[pl.ds(TAIL, TAIL_ROWS)], sems.at[6 + a]))
        for copy in edge_copies:
            copy.start()

        def apply(b, carry):
            rows = pl.ds(pl.multiple_of(b * BLOCK, BLOCK), BLOCK)
            w_new[rows, :] = news[0][rows, :] - rate_of(seg_map[rows, :]) * news[3][rows, :]
            return carry

        for p, (begin, end) in enumerate(BODY_PIECES):
            lax.fori_loop(begin, end, apply, 0, unroll=True)
            rows = pl.ds(begin * BLOCK, (end - begin) * BLOCK)
            body_copies.append(pltpu.make_async_copy(w_new.at[rows], w_out.at[rows], sems.at[9 + p]))
            body_copies[-1].start()
        for copy in body_copies + edge_copies:
            copy.wait()

    @pl.when(early)
    def _():
        emit((w_pre, m_pre, v_pre, u_pre), seg_pre)

    @pl.when(jnp.logical_not(early))
    def _():
        copy = pltpu.make_async_copy(seg_hbm, seg, seg_sem)
        copy.start()
        news = (w_late, m_late, v_late, u_late)
        move_interior(owns, news, shift)
        copy.wait()
        label_elements(seg_late, seg, low, low + count)
        emit(news, seg_late)


def in_hbm(*arrays):
    return [pltpu.with_memory_space_constraint(x, pltpu.HBM) for x in arrays]


def shards(params, first_moment, second_moment, grads, old_bounds, new_bounds, seg_start):
    hbm = pl.BlockSpec(memory_space=pltpu.HBM)
    vmem = pl.BlockSpec(memory_space=pltpu.VMEM)
    bounds = pltpu.SMEM((N_DP + 1,), jnp.int32)
    starts = pltpu.SMEM((SEGS,), jnp.int32)
    block_sums = pltpu.VMEM((BLOCKS * 8, LANES), jnp.float32)
    f32 = jnp.float32
    own = jax.ShapeDtypeStruct((PAD_ROWS, LANES), f32)
    rim = jax.ShapeDtypeStruct((4, RIM, LANES), f32)
    state = pltpu.VMEM((ROWS, LANES), f32)
    flat = [x.reshape(ROWS, LANES) for x in (params, first_moment, second_moment, grads)]
    moved = jax.ShapeDtypeStruct((ROWS, LANES), f32)
    labels = jax.ShapeDtypeStruct((ROWS, LANES), jnp.int32)
    pay, w_own, m_own, v_own, u_own, send_core, send_next, *early = pl.pallas_call(
        prepare,
        out_shape=(jax.ShapeDtypeStruct((N_DP, LANES), f32), own, own, own, own, rim, rim,
                   moved, moved, moved, moved, labels, jax.ShapeDtypeStruct((8, LANES), jnp.int32)),
        in_specs=[hbm] * 7,
        out_specs=[vmem] * 13,
        scratch_shapes=[state, state, pltpu.VMEM((ROWS, LANES), jnp.bfloat16), block_sums, block_sums,
                        pltpu.VMEM((2 * SEGS, LANES), f32), bounds, bounds, starts,
                        pltpu.SemaphoreType.DMA((4, 4)), pltpu.SemaphoreType.DMA((3,))],
        compiler_params=pltpu.CompilerParams(vmem_limit_bytes=24 * 2**20),
    )(*in_hbm(*flat, old_bounds, new_bounds, seg_start))
    pairs = [(i, i ^ 1) for i in range(N_DP)]
    between = [(i, (i + (1 if i % 2 else -1)) % N_DP) for i in range(N_DP)]
    from_next = lax.ppermute(send_next, "dp", between)
    from_core = lax.ppermute(send_core, "dp", pairs)
    parts = lax.all_to_all(pay, "dp", 0, 0, tiled=True)
    outs = pl.pallas_call(
        finish,
        out_shape=(jax.ShapeDtypeStruct((ROWS, LANES), f32),) * 3,
        in_specs=[vmem] * 13 + [hbm],
        out_specs=[hbm] * 3,
        scratch_shapes=[state] * 4 + [pltpu.VMEM((ROWS, LANES), jnp.int32), state]
        + [pltpu.VMEM((4, 136, LANES), f32), pltpu.VMEM((4, 136, LANES), f32), pltpu.VMEM((4, 48, LANES), f32),
           starts, pltpu.SemaphoreType.DMA((12,)), pltpu.SemaphoreType.DMA],
        compiler_params=pltpu.CompilerParams(vmem_limit_bytes=24 * 2**20),
    )(parts, w_own, m_own, v_own, u_own, from_next, from_core, *early, *in_hbm(seg_start))
    return tuple(x.reshape(-1) for x in outs)


def solution(mesh):
    return jax.shard_map(
        shards,
        mesh=mesh,
        in_specs=(P("dp"), P("dp"), P("dp"), P("dp"), P(), P(), P()),
        out_specs=(P("dp"), P("dp"), P("dp")),
        check_vma=False,
    )
```

```python
import jax
import jax.numpy as jnp
from jax import lax
from jax.experimental import pallas as pl
from jax.experimental.pallas import tpu as pltpu
from jax.sharding import PartitionSpec as P

MARGIN = 4096
SEGS = 64
N_DP = 128
LANES = 128
ROWS = 992
RIM = MARGIN // LANES
PAD_ROWS = 1032
TAIL = 896
TAIL_ROWS = ROWS - TAIL
BODY_PIECES = ((1, 14), (14, 22), (22, 28))

BETA_ONE = 0.9
BETA_TWO = 0.999
CORR_ONE = 1.0 - 0.9**10
CORR_TWO = 1.0 - 0.999**10
DECAY = 0.01
LEARN = 0.1
EPSILON = 1e-06

BLOCK = 32
BLOCK_ELEMS = BLOCK * LANES
BLOCKS = ROWS // BLOCK
PIECES = ((0, 8), (8, 16), (16, 24), (24, 31))


def lanes_of(rows):
    return lax.broadcasted_iota(jnp.int32, (rows, LANES), 1)


def index_of(rows):
    return lax.broadcasted_iota(jnp.int32, (rows, LANES), 0) * LANES + lanes_of(rows)


def segment_range(seg, low, high):
    first = jnp.int32(0)
    last = jnp.int32(0)
    for step in (32, 16, 8, 4, 2, 1):
        first = first + jnp.where(seg[first + step] <= low, step, 0)
        last = last + jnp.where(seg[last + step] < high, step, 0)
    return first, last


def segment_span(seg, s, low, high):
    begin = jnp.maximum(seg[s], low) - low
    following = jnp.where(s == SEGS - 1, high, seg[jnp.minimum(s + 1, SEGS - 1)])
    end = jnp.minimum(following, high) - low
    return begin, end


def is_early(device):
    return (device // 8 % 4 + device // 32 <= 1) & (device % 8 < 4)


def move_interior(owns, news, shift):
    shift_row = shift // LANES
    shift_lane = lax.rem(shift, LANES)
    back = lax.rem(LANES - shift_lane, LANES)
    keep = lanes_of(BLOCK) >= shift_lane

    def move(b, carry):
        source = b * BLOCK + shift_row - RIM
        rows = pl.ds(pl.multiple_of(b * BLOCK, BLOCK), BLOCK)
        for own, fresh in zip(owns, news):
            here = own[pl.ds(source, BLOCK), :]
            below = own[pl.ds(source + 1, BLOCK), :]
            fresh[rows, :] = pltpu.roll(jnp.where(keep, here, below), back, 1)
        return carry

    lax.fori_loop(1, BLOCKS, move, 0, unroll=True)


def label_elements(seg_map, seg, low, high):
    first, last = segment_range(seg, low, high)
    element = index_of(BLOCK)

    def segment(s, carry):
        begin, end = segment_span(seg, s, low, high)
        first_block = begin // BLOCK_ELEMS
        last_block = jnp.where(s == last, BLOCKS - 1, (end - 1) // BLOCK_ELEMS)
        rows = pl.ds(pl.multiple_of(first_block * BLOCK, BLOCK), BLOCK)
        seg_map[rows, :] = jnp.where(element + first_block * BLOCK_ELEMS >= begin, s, seg_map[rows, :])

        def fill(b, inner):
            seg_map[pl.ds(pl.multiple_of(b * BLOCK, BLOCK), BLOCK), :] = jnp.full((BLOCK, LANES), s, jnp.int32)
            return inner

        lax.fori_loop(first_block + 1, last_block + 1, fill, 0)
        return carry

    lax.fori_loop(first, last + 1, segment, 0)


def fold(x):
    return x[0:8] + x[8:16] + x[16:24] + x[24:32]


def prepare(w_hbm, m_hbm, v_hbm, g_hbm, old_hbm, new_hbm, seg_hbm,
            pay, w_own, m_own, v_own, u_own, send_core, send_next, w_new, m_new, v_new, u_new, seg_map, info,
            m_in, v_in, g_in, weight_sums, update_sums, table, old, new, seg, sems, scalar_sems):
    scalar_copies = [
        pltpu.make_async_copy(old_hbm, old, scalar_sems.at[0]),
        pltpu.make_async_copy(seg_hbm, seg, scalar_sems.at[1]),
        pltpu.make_async_copy(new_hbm, new, scalar_sems.at[2]),
    ]
    for copy in scalar_copies:
        copy.start()
    pieces = []
    for p, (begin, end) in enumerate(PIECES):
        rows = pl.ds(begin * BLOCK, (end - begin) * BLOCK)
        pieces.append([
            pltpu.make_async_copy(source.at[rows], target.at[rows], sems.at[p, a])
            for a, (source, target) in enumerate(((g_hbm, g_in), (v_hbm, v_in), (m_hbm, m_in), (w_hbm, w_own)))
        ])
        for copy in pieces[-1]:
            copy.start()
    device = lax.axis_index("dp")
    even = lax.rem(device, 2) == 0
    for copy in scalar_copies:
        copy.wait()
    low = old[device]
    high = old[device + 1]
    count = high - low
    new_low = new[device]
    new_high = new[device + 1]
    row = lax.broadcasted_iota(jnp.int32, (8, LANES), 0)
    facts = jnp.where(row == 0, new_low - low + MARGIN, new_low)
    facts = jnp.where(row == 1, high - new_low, facts)
    info[...] = jnp.where(row == 2, new_high - new_low, facts)
    first, last = segment_range(seg, low, high)

    def update(b, carry):
        rows = pl.ds(pl.multiple_of(b * BLOCK, BLOCK), BLOCK)
        grad = g_in[rows, :].astype(jnp.float32)
        weight = w_own[rows, :]
        moment = BETA_ONE * m_in[rows, :] + (1.0 - BETA_ONE) * grad
        second = BETA_TWO * v_in[rows, :] + (1.0 - BETA_TWO) * grad * grad
        step = moment * (1.0 / CORR_ONE) / (jnp.sqrt(second * (1.0 / CORR_TWO)) + EPSILON) + DECAY * weight
        m_own[rows, :] = moment
        v_own[rows, :] = second
        u_own[rows, :] = step
        short = pl.ds(pl.multiple_of(b * 8, 8), 8)
        weight_sums[short, :] = fold(weight * weight)
        update_sums[short, :] = fold(step * step)
        return carry

    for (begin, end), copies in zip(PIECES, pieces):
        for copy in copies:
            copy.wait()
        lax.fori_loop(begin, end, update, 0, unroll=True)

    cut = count - MARGIN
    cut_row = cut // LANES
    cut_lane = lax.rem(cut, LANES)
    back = lax.rem(LANES - cut_lane, LANES)
    for a, source in enumerate((w_own, m_own, v_own, u_own)):
        here = source[pl.ds(cut_row, RIM), :]
        below = source[pl.ds(cut_row + 1, RIM), :]
        tail = pltpu.roll(jnp.where(lanes_of(RIM) >= cut_lane, here, below), back, 1)
        head = source[pl.ds(0, RIM), :]
        send_next[a] = jnp.where(even, head, tail)
        send_core[a] = jnp.where(even, tail, head)

    element = index_of(BLOCK)

    lane = lanes_of(8)

    def segment(s, packed):
        begin, end = segment_span(seg, s, low, high)
        first_block = begin // BLOCK_ELEMS
        last_block = (end - 1) // BLOCK_ELEMS

        def edge(b, sums):
            weight_sum, update_sum = sums
            rows = pl.ds(pl.multiple_of(b * BLOCK, BLOCK), BLOCK)
            place = element + b * BLOCK_ELEMS
            inside = (place >= begin) & (place < end)
            weight = w_own[rows, :]
            step = u_own[rows, :]
            weight_sum = weight_sum + fold(jnp.where(inside, weight * weight, 0.0))
            update_sum = update_sum + fold(jnp.where(inside, step * step, 0.0))
            return weight_sum, update_sum

        def whole(group, sums):
            weight_sum, update_sum = sums
            for b in range(8):
                block = group * 8 + b
                inner = (block > first_block) & (block < last_block)
                short = pl.ds(pl.multiple_of(group * 64 + b * 8, 8), 8)
                weight_sum = weight_sum + jnp.where(inner, weight_sums[short, :], 0.0)
                update_sum = update_sum + jnp.where(inner, update_sums[short, :], 0.0)
            return weight_sum, update_sum

        zero = jnp.zeros((8, LANES), jnp.float32)
        sums = edge(first_block, (zero, zero))
        sums = lax.fori_loop((first_block + 1) // 8, (last_block + 7) // 8, whole, sums)
        weight_sum, update_sum = lax.fori_loop(jnp.maximum(last_block, first_block + 1), last_block + 1, edge, sums)
        weight_sum = jnp.sum(jnp.sum(weight_sum, axis=0, keepdims=True), axis=1, keepdims=True)
        update_sum = jnp.sum(jnp.sum(update_sum, axis=0, keepdims=True), axis=1, keepdims=True)
        return packed + jnp.where(lane == s, weight_sum, 0.0) + jnp.where(lane == SEGS + s, update_sum, 0.0)

    packed = lax.fori_loop(first, last + 1, segment, jnp.zeros((8, LANES), jnp.float32))
    for row in range(0, N_DP, 8):
        pay[pl.ds(row, 8), :] = packed

    @pl.when(is_early(device))
    def _():
        move_interior((w_own, m_own, v_own, u_own), (w_new, m_new, v_new, u_new), new_low - low + MARGIN)
        label_elements(seg_map, seg, new_low, new_high)


def finish(parts, w_own, m_own, v_own, u_own, from_next, from_core, w_pre, m_pre, v_pre, u_pre, seg_pre,
           info, seg_hbm, w_out, m_out, v_out,
           w_late, m_late, v_late, u_late, seg_late, w_new, heads, tails, rims, seg, sems, seg_sem):
    device = lax.axis_index("dp")
    facts = info[...]
    shift = facts[0, 0]
    cut = facts[1, 0]
    count = facts[2, 0]
    low = facts[3, 0]
    early = is_early(device)
    owns = (w_own, m_own, v_own, u_own)
    outs = (w_out, m_out, v_out)
    body = pl.ds(RIM, TAIL - RIM)

    def emit(news, seg_map):
        body_copies = [pltpu.make_async_copy(news[a].at[body], outs[a].at[body], sems.at[a]) for a in (1, 2)]
        for copy in body_copies:
            copy.start()
        sums = jnp.broadcast_to(jnp.sum(parts[...], axis=0, keepdims=True), (8, LANES))
        rates = LEARN * jnp.sqrt(sums) / (jnp.sqrt(pltpu.roll(sums, SEGS, 1)) + EPSILON)

        def rate_of(labels):
            pieces = [jnp.take_along_axis(rates, labels[r:r + 8], axis=1) for r in range(0, labels.shape[0], 8)]
            return jnp.concatenate(pieces, axis=0)

        def apply(b, carry):
            rows = pl.ds(pl.multiple_of(b * BLOCK, BLOCK), BLOCK)
            w_new[rows, :] = news[0][rows, :] - rate_of(seg_map[rows, :]) * news[3][rows, :]
            return carry

        for p, (begin, end) in enumerate(BODY_PIECES):
            lax.fori_loop(begin, end, apply, 0, unroll=True)
            rows = pl.ds(begin * BLOCK, (end - begin) * BLOCK)
            body_copies.append(pltpu.make_async_copy(w_new.at[rows], w_out.at[rows], sems.at[9 + p]))
            body_copies[-1].start()
        shift_row = shift // LANES
        shift_lane = lax.rem(shift, LANES)
        back = lax.rem(LANES - shift_lane, LANES)
        even = lax.rem(device, 2) == 0

        for a in range(4):
            heads[a, pl.ds(0, RIM), :] = jnp.where(even, from_next[a], from_core[a])
            rims[a, pl.ds(8, RIM), :] = jnp.where(even, from_core[a], from_next[a])

        keep = lanes_of(RIM) >= shift_lane
        tail_live = index_of(TAIL_ROWS) + TAIL * LANES < count
        for a in range(4):
            heads[a, pl.ds(RIM, 72), :] = owns[a][pl.ds(0, 72), :]
            here = heads[a, pl.ds(shift_row, RIM), :]
            below = heads[a, pl.ds(shift_row + 1, RIM), :]
            heads[a, pl.ds(104, RIM), :] = pltpu.roll(jnp.where(keep, here, below), back, 1)
            tails[a, pl.ds(0, TAIL_ROWS), :] = jnp.where(tail_live, news[a][pl.ds(TAIL, TAIL_ROWS), :], 0.0)

        cut_row = jnp.minimum(cut // LANES - TAIL, TAIL_ROWS)
        cut_lane = lax.rem(cut, LANES)
        place = index_of(40) + (cut_row + TAIL) * LANES
        taken = (place >= cut) & (place < count)
        fits = lanes_of(40) < LANES - cut_lane
        rows = pl.ds(cut_row, 40)
        for a in range(4):
            here = rims[a, pl.ds(8, 40), :]
            above = rims[a, pl.ds(7, 40), :]
            incoming = pltpu.roll(jnp.where(fits, here, above), cut_lane, 1)
            tails[a, rows, :] = jnp.where(taken, incoming, tails[a, rows, :])

        top = pl.ds(104, RIM)
        heads[0, top, :] = heads[0, top, :] - rate_of(seg_map[pl.ds(0, RIM), :]) * heads[3, top, :]
        bottom = pl.ds(0, TAIL_ROWS)
        tails[0, bottom, :] = tails[0, bottom, :] - rate_of(seg_map[pl.ds(TAIL, TAIL_ROWS), :]) * tails[3, bottom, :]
        edge_copies = []
        for a in range(3):
            edge_copies.append(pltpu.make_async_copy(heads.at[a, top], outs[a].at[pl.ds(0, RIM)], sems.at[3 + a]))
            edge_copies.append(
                pltpu.make_async_copy(tails.at[a, bottom], outs[a].at[pl.ds(TAIL, TAIL_ROWS)], sems.at[6 + a]))
        for copy in edge_copies:
            copy.start()

        for copy in body_copies + edge_copies:
            copy.wait()

    @pl.when(early)
    def _():
        emit((w_pre, m_pre, v_pre, u_pre), seg_pre)

    @pl.when(jnp.logical_not(early))
    def _():
        copy = pltpu.make_async_copy(seg_hbm, seg, seg_sem)
        copy.start()
        news = (w_late, m_late, v_late, u_late)
        move_interior(owns, news, shift)
        copy.wait()
        label_elements(seg_late, seg, low, low + count)
        emit(news, seg_late)


def in_hbm(*arrays):
    return [pltpu.with_memory_space_constraint(x, pltpu.HBM) for x in arrays]


def shards(params, first_moment, second_moment, grads, old_bounds, new_bounds, seg_start):
    hbm = pl.BlockSpec(memory_space=pltpu.HBM)
    vmem = pl.BlockSpec(memory_space=pltpu.VMEM)
    bounds = pltpu.SMEM((N_DP + 1,), jnp.int32)
    starts = pltpu.SMEM((SEGS,), jnp.int32)
    block_sums = pltpu.VMEM((32 * 8, LANES), jnp.float32)
    f32 = jnp.float32
    own = jax.ShapeDtypeStruct((PAD_ROWS, LANES), f32)
    rim = jax.ShapeDtypeStruct((4, RIM, LANES), f32)
    state = pltpu.VMEM((ROWS, LANES), f32)
    flat = [x.reshape(ROWS, LANES) for x in (params, first_moment, second_moment, grads)]
    moved = jax.ShapeDtypeStruct((ROWS, LANES), f32)
    labels = jax.ShapeDtypeStruct((ROWS, LANES), jnp.int32)
    pay, w_own, m_own, v_own, u_own, send_core, send_next, *early = pl.pallas_call(
        prepare,
        out_shape=(jax.ShapeDtypeStruct((N_DP, LANES), f32), own, own, own, own, rim, rim,
                   moved, moved, moved, moved, labels, jax.ShapeDtypeStruct((8, LANES), jnp.int32)),
        in_specs=[hbm] * 7,
        out_specs=[vmem] * 13,
        scratch_shapes=[state, state, pltpu.VMEM((ROWS, LANES), jnp.bfloat16), block_sums, block_sums,
                        pltpu.VMEM((2 * SEGS, LANES), f32), bounds, bounds, starts,
                        pltpu.SemaphoreType.DMA((4, 4)), pltpu.SemaphoreType.DMA((3,))],
        compiler_params=pltpu.CompilerParams(vmem_limit_bytes=24 * 2**20),
    )(*in_hbm(*flat, old_bounds, new_bounds, seg_start))
    pairs = [(i, i ^ 1) for i in range(N_DP)]
    between = [(i, (i + (1 if i % 2 else -1)) % N_DP) for i in range(N_DP)]
    from_next = lax.ppermute(send_next, "dp", between)
    from_core = lax.ppermute(send_core, "dp", pairs)
    parts = lax.all_to_all(pay, "dp", 0, 0, tiled=True)
    outs = pl.pallas_call(
        finish,
        out_shape=(jax.ShapeDtypeStruct((ROWS, LANES), f32),) * 3,
        in_specs=[vmem] * 13 + [hbm],
        out_specs=[hbm] * 3,
        scratch_shapes=[state] * 4 + [pltpu.VMEM((ROWS, LANES), jnp.int32), state]
        + [pltpu.VMEM((4, 136, LANES), f32), pltpu.VMEM((4, 136, LANES), f32), pltpu.VMEM((4, 48, LANES), f32),
           starts, pltpu.SemaphoreType.DMA((12,)), pltpu.SemaphoreType.DMA],
        compiler_params=pltpu.CompilerParams(vmem_limit_bytes=24 * 2**20),
    )(parts, w_own, m_own, v_own, u_own, from_next, from_core, *early, *in_hbm(seg_start))
    return tuple(x.reshape(-1) for x in outs)


def solution(mesh):
    return jax.shard_map(
        shards,
        mesh=mesh,
        in_specs=(P("dp"), P("dp"), P("dp"), P("dp"), P(), P(), P()),
        out_specs=(P("dp"), P("dp"), P("dp")),
        check_vma=False,
    )
```

```python
import jax
import jax.numpy as jnp
from jax import lax
from jax.experimental import pallas as pl
from jax.experimental.pallas import tpu as pltpu
from jax.sharding import PartitionSpec as P

MARGIN = 4096
SEGS = 64
N_DP = 128
LANES = 128
ROWS = 992
RIM = MARGIN // LANES
PAD_ROWS = 1032
TAIL = 896
TAIL_ROWS = ROWS - TAIL
BODY_PIECES = ((1, 14), (14, 22), (22, 28))

BETA_ONE = 0.9
BETA_TWO = 0.999
CORR_ONE = 1.0 - 0.9**10
CORR_TWO = 1.0 - 0.999**10
DECAY = 0.01
LEARN = 0.1
EPSILON = 1e-06

BLOCK = 32
BLOCK_ELEMS = BLOCK * LANES
BLOCKS = ROWS // BLOCK
LIVE = 29
PIECES = ((0, 8), (8, 16), (16, 24), (24, 31))


def lanes_of(rows):
    return lax.broadcasted_iota(jnp.int32, (rows, LANES), 1)


def index_of(rows):
    return lax.broadcasted_iota(jnp.int32, (rows, LANES), 0) * LANES + lanes_of(rows)


def segment_range(seg, low, high):
    first = jnp.int32(0)
    last = jnp.int32(0)
    for step in (32, 16, 8, 4, 2, 1):
        first = first + jnp.where(seg[first + step] <= low, step, 0)
        last = last + jnp.where(seg[last + step] < high, step, 0)
    return first, last


def segment_span(seg, s, low, high):
    begin = jnp.maximum(seg[s], low) - low
    following = jnp.where(s == SEGS - 1, high, seg[jnp.minimum(s + 1, SEGS - 1)])
    end = jnp.minimum(following, high) - low
    return begin, end


def is_early(device):
    return (device // 8 % 4 + device // 32 <= 1) & (device % 8 < 4)


def move_interior(owns, news, shift):
    shift_row = shift // LANES
    shift_lane = lax.rem(shift, LANES)
    back = lax.rem(LANES - shift_lane, LANES)
    keep = lanes_of(BLOCK) >= shift_lane

    def move(b, carry):
        source = b * BLOCK + shift_row - RIM
        rows = pl.ds(pl.multiple_of(b * BLOCK, BLOCK), BLOCK)
        for own, fresh in zip(owns, news):
            here = own[pl.ds(source, BLOCK), :]
            below = own[pl.ds(source + 1, BLOCK), :]
            fresh[rows, :] = pltpu.roll(jnp.where(keep, here, below), back, 1)
        return carry

    lax.fori_loop(1, BLOCKS, move, 0, unroll=True)


def label_elements(seg_map, seg, low, high):
    first, last = segment_range(seg, low, high)
    element = index_of(BLOCK)

    def segment(s, carry):
        begin, end = segment_span(seg, s, low, high)
        first_block = begin // BLOCK_ELEMS
        last_block = jnp.where(s == last, BLOCKS - 1, (end - 1) // BLOCK_ELEMS)
        rows = pl.ds(pl.multiple_of(first_block * BLOCK, BLOCK), BLOCK)
        seg_map[rows, :] = jnp.where(element + first_block * BLOCK_ELEMS >= begin, s, seg_map[rows, :])

        def fill(b, inner):
            seg_map[pl.ds(pl.multiple_of(b * BLOCK, BLOCK), BLOCK), :] = jnp.full((BLOCK, LANES), s, jnp.int32)
            return inner

        lax.fori_loop(first_block + 1, last_block + 1, fill, 0)
        return carry

    lax.fori_loop(first, last + 1, segment, 0)


def fold(x):
    return x[0:8] + x[8:16] + x[16:24] + x[24:32]


def prepare(w_hbm, m_hbm, v_hbm, g_hbm, old_hbm, new_hbm, seg_hbm,
            pay, w_own, m_own, v_own, u_own, send_core, send_next, w_new, m_new, v_new, u_new, seg_map, info,
            m_in, v_in, g_in, weight_sums, update_sums, old, new, seg, sems, scalar_sems):
    scalar_copies = [
        pltpu.make_async_copy(old_hbm, old, scalar_sems.at[0]),
        pltpu.make_async_copy(seg_hbm, seg, scalar_sems.at[1]),
        pltpu.make_async_copy(new_hbm, new, scalar_sems.at[2]),
    ]
    for copy in scalar_copies:
        copy.start()
    pieces = []
    for p, (begin, end) in enumerate(PIECES):
        rows = pl.ds(begin * BLOCK, (end - begin) * BLOCK)
        pieces.append([
            pltpu.make_async_copy(source.at[rows], target.at[rows], sems.at[p, a])
            for a, (source, target) in enumerate(((g_hbm, g_in), (v_hbm, v_in), (m_hbm, m_in), (w_hbm, w_own)))
        ])
        for copy in pieces[-1]:
            copy.start()
    device = lax.axis_index("dp")
    even = lax.rem(device, 2) == 0
    for copy in scalar_copies:
        copy.wait()
    low = old[device]
    high = old[device + 1]
    count = high - low
    new_low = new[device]
    new_high = new[device + 1]
    row = lax.broadcasted_iota(jnp.int32, (8, LANES), 0)
    facts = jnp.where(row == 0, new_low - low + MARGIN, new_low)
    facts = jnp.where(row == 1, high - new_low, facts)
    info[...] = jnp.where(row == 2, new_high - new_low, facts)
    first, last = segment_range(seg, low, high)

    def update(b, carry):
        rows = pl.ds(pl.multiple_of(b * BLOCK, BLOCK), BLOCK)
        grad = g_in[rows, :].astype(jnp.float32)
        weight = w_own[rows, :]
        moment = BETA_ONE * m_in[rows, :] + (1.0 - BETA_ONE) * grad
        second = BETA_TWO * v_in[rows, :] + (1.0 - BETA_TWO) * grad * grad
        step = moment * (1.0 / CORR_ONE) / (jnp.sqrt(second * (1.0 / CORR_TWO)) + EPSILON) + DECAY * weight
        m_own[rows, :] = moment
        v_own[rows, :] = second
        u_own[rows, :] = step
        short = pl.ds(pl.multiple_of(b * 8, 8), 8)
        weight_sum = fold(weight * weight)
        update_sum = fold(step * step)
        weight_sums[short, :] = weight_sum
        update_sums[short, :] = update_sum
        return carry[0] + weight_sum, carry[1] + update_sum

    zero = jnp.zeros((8, LANES), jnp.float32)
    live_sums = (zero, zero)
    for (begin, end), copies in zip(PIECES, pieces):
        for copy in copies:
            copy.wait()
        live_sums = lax.fori_loop(begin, min(end, LIVE), update, live_sums, unroll=True)
        lax.fori_loop(min(end, LIVE), end, update, (zero, zero), unroll=True)

    cut = count - MARGIN
    cut_row = cut // LANES
    cut_lane = lax.rem(cut, LANES)
    back = lax.rem(LANES - cut_lane, LANES)
    for a, source in enumerate((w_own, m_own, v_own, u_own)):
        here = source[pl.ds(cut_row, RIM), :]
        below = source[pl.ds(cut_row + 1, RIM), :]
        tail = pltpu.roll(jnp.where(lanes_of(RIM) >= cut_lane, here, below), back, 1)
        head = source[pl.ds(0, RIM), :]
        send_next[a] = jnp.where(even, head, tail)
        send_core[a] = jnp.where(even, tail, head)

    element = index_of(BLOCK)

    lane = lanes_of(8)

    def masked(b, sums, begin, end):
        weight_sum, update_sum = sums
        rows = pl.ds(pl.multiple_of(b * BLOCK, BLOCK), BLOCK)
        place = element + b * BLOCK_ELEMS
        inside = (place >= begin) & (place < end)
        weight = w_own[rows, :]
        step = u_own[rows, :]
        weight_sum = weight_sum + fold(jnp.where(inside, weight * weight, 0.0))
        update_sum = update_sum + fold(jnp.where(inside, step * step, 0.0))
        return weight_sum, update_sum

    def pack(s, weight_sum, update_sum):
        weight_sum = jnp.sum(jnp.sum(weight_sum, axis=0, keepdims=True), axis=1, keepdims=True)
        update_sum = jnp.sum(jnp.sum(update_sum, axis=0, keepdims=True), axis=1, keepdims=True)
        return jnp.where(lane == s, weight_sum, 0.0) + jnp.where(lane == SEGS + s, update_sum, 0.0)

    def segment(s, packed):
        begin, end = segment_span(seg, s, low, high)
        first_block = begin // BLOCK_ELEMS
        last_block = (end - 1) // BLOCK_ELEMS

        def edge(b, sums):
            return masked(b, sums, begin, end)

        def whole(group, sums):
            weight_sum, update_sum = sums
            for b in range(8):
                block = group * 8 + b
                inner = (block > first_block) & (block < last_block)
                short = pl.ds(pl.multiple_of(group * 64 + b * 8, 8), 8)
                weight_sum = weight_sum + jnp.where(inner, weight_sums[short, :], 0.0)
                update_sum = update_sum + jnp.where(inner, update_sums[short, :], 0.0)
            return weight_sum, update_sum

        sums = edge(first_block, (zero, zero))
        sums = lax.fori_loop((first_block + 1) // 8, (last_block + 7) // 8, whole, sums)
        sums = lax.fori_loop(jnp.maximum(last_block, first_block + 1), last_block + 1, edge, sums)
        return packed + pack(s, *sums)

    def one_tensor():
        sums = live_sums
        for b in range(LIVE, BLOCKS):
            sums = masked(b, sums, 0, count)
        return pack(first, *sums)

    def several_tensors():
        return lax.fori_loop(first, last + 1, segment, jnp.zeros((8, LANES), jnp.float32))

    packed = lax.cond(first == last, one_tensor, several_tensors)
    for row in range(0, N_DP, 8):
        pay[pl.ds(row, 8), :] = packed

    @pl.when(is_early(device))
    def _():
        move_interior((w_own, m_own, v_own, u_own), (w_new, m_new, v_new, u_new), new_low - low + MARGIN)
        label_elements(seg_map, seg, new_low, new_high)


def finish(parts, w_own, m_own, v_own, u_own, from_next, from_core, w_pre, m_pre, v_pre, u_pre, seg_pre,
           info, seg_hbm, w_out, m_out, v_out,
           w_late, m_late, v_late, u_late, seg_late, w_new, heads, tails, rims, seg, sems, seg_sem):
    device = lax.axis_index("dp")
    facts = info[...]
    shift = facts[0, 0]
    cut = facts[1, 0]
    count = facts[2, 0]
    low = facts[3, 0]
    early = is_early(device)
    owns = (w_own, m_own, v_own, u_own)
    outs = (w_out, m_out, v_out)
    body = pl.ds(RIM, TAIL - RIM)

    def emit(news, seg_map):
        body_copies = [pltpu.make_async_copy(news[a].at[body], outs[a].at[body], sems.at[a]) for a in (1, 2)]
        for copy in body_copies:
            copy.start()
        sums = jnp.broadcast_to(jnp.sum(parts[...], axis=0, keepdims=True), (8, LANES))
        roots = jnp.sqrt(sums)
        rates = LEARN * roots / (pltpu.roll(roots, SEGS, 1) + EPSILON)

        def rate_of(labels):
            pieces = [jnp.take_along_axis(rates, labels[r:r + 8], axis=1) for r in range(0, labels.shape[0], 8)]
            return jnp.concatenate(pieces, axis=0)

        def apply(b, carry):
            rows = pl.ds(pl.multiple_of(b * BLOCK, BLOCK), BLOCK)
            w_new[rows, :] = news[0][rows, :] - rate_of(seg_map[rows, :]) * news[3][rows, :]
            return carry

        for p, (begin, end) in enumerate(BODY_PIECES):
            lax.fori_loop(begin, end, apply, 0, unroll=True)
            rows = pl.ds(begin * BLOCK, (end - begin) * BLOCK)
            body_copies.append(pltpu.make_async_copy(w_new.at[rows], w_out.at[rows], sems.at[9 + p]))
            body_copies[-1].start()
        shift_row = shift // LANES
        shift_lane = lax.rem(shift, LANES)
        back = lax.rem(LANES - shift_lane, LANES)
        even = lax.rem(device, 2) == 0

        for a in range(4):
            heads[a, pl.ds(0, RIM), :] = jnp.where(even, from_next[a], from_core[a])
            rims[a, pl.ds(8, RIM), :] = jnp.where(even, from_core[a], from_next[a])

        keep = lanes_of(RIM) >= shift_lane
        tail_live = index_of(TAIL_ROWS) + TAIL * LANES < count
        for a in range(4):
            heads[a, pl.ds(RIM, 72), :] = owns[a][pl.ds(0, 72), :]
            here = heads[a, pl.ds(shift_row, RIM), :]
            below = heads[a, pl.ds(shift_row + 1, RIM), :]
            heads[a, pl.ds(104, RIM), :] = pltpu.roll(jnp.where(keep, here, below), back, 1)
            tails[a, pl.ds(0, TAIL_ROWS), :] = jnp.where(tail_live, news[a][pl.ds(TAIL, TAIL_ROWS), :], 0.0)

        cut_row = jnp.minimum(cut // LANES - TAIL, TAIL_ROWS)
        cut_lane = lax.rem(cut, LANES)
        place = index_of(40) + (cut_row + TAIL) * LANES
        taken = (place >= cut) & (place < count)
        fits = lanes_of(40) < LANES - cut_lane
        rows = pl.ds(cut_row, 40)
        for a in range(4):
            here = rims[a, pl.ds(8, 40), :]
            above = rims[a, pl.ds(7, 40), :]
            incoming = pltpu.roll(jnp.where(fits, here, above), cut_lane, 1)
            tails[a, rows, :] = jnp.where(taken, incoming, tails[a, rows, :])

        top = pl.ds(104, RIM)
        heads[0, top, :] = heads[0, top, :] - rate_of(seg_map[pl.ds(0, RIM), :]) * heads[3, top, :]
        bottom = pl.ds(0, TAIL_ROWS)
        tails[0, bottom, :] = tails[0, bottom, :] - rate_of(seg_map[pl.ds(TAIL, TAIL_ROWS), :]) * tails[3, bottom, :]
        edge_copies = []
        for a in range(3):
            edge_copies.append(pltpu.make_async_copy(heads.at[a, top], outs[a].at[pl.ds(0, RIM)], sems.at[3 + a]))
            edge_copies.append(
                pltpu.make_async_copy(tails.at[a, bottom], outs[a].at[pl.ds(TAIL, TAIL_ROWS)], sems.at[6 + a]))
        for copy in edge_copies:
            copy.start()

        for copy in body_copies + edge_copies:
            copy.wait()

    @pl.when(early)
    def _():
        emit((w_pre, m_pre, v_pre, u_pre), seg_pre)

    @pl.when(jnp.logical_not(early))
    def _():
        copy = pltpu.make_async_copy(seg_hbm, seg, seg_sem)
        copy.start()
        news = (w_late, m_late, v_late, u_late)
        move_interior(owns, news, shift)
        copy.wait()
        label_elements(seg_late, seg, low, low + count)
        emit(news, seg_late)


def in_hbm(*arrays):
    return [pltpu.with_memory_space_constraint(x, pltpu.HBM) for x in arrays]


def shards(params, first_moment, second_moment, grads, old_bounds, new_bounds, seg_start):
    hbm = pl.BlockSpec(memory_space=pltpu.HBM)
    vmem = pl.BlockSpec(memory_space=pltpu.VMEM)
    bounds = pltpu.SMEM((N_DP + 1,), jnp.int32)
    starts = pltpu.SMEM((SEGS,), jnp.int32)
    block_sums = pltpu.VMEM((32 * 8, LANES), jnp.float32)
    f32 = jnp.float32
    own = jax.ShapeDtypeStruct((PAD_ROWS, LANES), f32)
    rim = jax.ShapeDtypeStruct((4, RIM, LANES), f32)
    state = pltpu.VMEM((ROWS, LANES), f32)
    flat = [x.reshape(ROWS, LANES) for x in (params, first_moment, second_moment, grads)]
    moved = jax.ShapeDtypeStruct((ROWS, LANES), f32)
    labels = jax.ShapeDtypeStruct((ROWS, LANES), jnp.int32)
    pay, w_own, m_own, v_own, u_own, send_core, send_next, *early = pl.pallas_call(
        prepare,
        out_shape=(jax.ShapeDtypeStruct((N_DP, LANES), f32), own, own, own, own, rim, rim,
                   moved, moved, moved, moved, labels, jax.ShapeDtypeStruct((8, LANES), jnp.int32)),
        in_specs=[hbm] * 7,
        out_specs=[vmem] * 13,
        scratch_shapes=[state, state, pltpu.VMEM((ROWS, LANES), jnp.bfloat16), block_sums, block_sums,
                        bounds, bounds, starts,
                        pltpu.SemaphoreType.DMA((4, 4)), pltpu.SemaphoreType.DMA((3,))],
        compiler_params=pltpu.CompilerParams(vmem_limit_bytes=24 * 2**20),
    )(*in_hbm(*flat, old_bounds, new_bounds, seg_start))
    pairs = [(i, i ^ 1) for i in range(N_DP)]
    between = [(i, (i + (1 if i % 2 else -1)) % N_DP) for i in range(N_DP)]
    from_next = lax.ppermute(send_next, "dp", between)
    from_core = lax.ppermute(send_core, "dp", pairs)
    parts = lax.all_to_all(pay, "dp", 0, 0, tiled=True)
    outs = pl.pallas_call(
        finish,
        out_shape=(jax.ShapeDtypeStruct((ROWS, LANES), f32),) * 3,
        in_specs=[vmem] * 13 + [hbm],
        out_specs=[hbm] * 3,
        scratch_shapes=[state] * 4 + [pltpu.VMEM((ROWS, LANES), jnp.int32), state]
        + [pltpu.VMEM((4, 136, LANES), f32), pltpu.VMEM((4, 136, LANES), f32), pltpu.VMEM((4, 48, LANES), f32),
           starts, pltpu.SemaphoreType.DMA((12,)), pltpu.SemaphoreType.DMA],
        compiler_params=pltpu.CompilerParams(vmem_limit_bytes=24 * 2**20),
    )(parts, w_own, m_own, v_own, u_own, from_next, from_core, *early, *in_hbm(seg_start))
    return tuple(x.reshape(-1) for x in outs)


def solution(mesh):
    return jax.shard_map(
        shards,
        mesh=mesh,
        in_specs=(P("dp"), P("dp"), P("dp"), P("dp"), P(), P(), P()),
        out_specs=(P("dp"), P("dp"), P("dp")),
        check_vma=False,
    )
```

```python
import jax
import jax.numpy as jnp
from jax import lax
from jax.experimental import pallas as pl
from jax.experimental.pallas import tpu as pltpu
from jax.sharding import PartitionSpec as P

MARGIN = 4096
SEGS = 64
N_DP = 128
LANES = 128
ROWS = 992
RIM = MARGIN // LANES
PAD_ROWS = 1032
TAIL = 896
TAIL_ROWS = ROWS - TAIL
BODY_PIECES = ((1, 8), (8, 15), (15, 22), (22, 28))

BETA_ONE = 0.9
BETA_TWO = 0.999
CORR_ONE = 1.0 - 0.9**10
CORR_TWO = 1.0 - 0.999**10
DECAY = 0.01
LEARN = 0.1
EPSILON = 1e-06

BLOCK = 32
BLOCK_ELEMS = BLOCK * LANES
BLOCKS = ROWS // BLOCK
LIVE = 29
PIECES = ((0, 8), (8, 16), (16, 24), (24, 31))


def lanes_of(rows):
    return lax.broadcasted_iota(jnp.int32, (rows, LANES), 1)


def index_of(rows):
    return lax.broadcasted_iota(jnp.int32, (rows, LANES), 0) * LANES + lanes_of(rows)


def segment_range(seg, low, high):
    first = jnp.int32(0)
    last = jnp.int32(0)
    for step in (32, 16, 8, 4, 2, 1):
        first = first + jnp.where(seg[first + step] <= low, step, 0)
        last = last + jnp.where(seg[last + step] < high, step, 0)
    return first, last


def segment_span(seg, s, low, high):
    begin = jnp.maximum(seg[s], low) - low
    following = jnp.where(s == SEGS - 1, high, seg[jnp.minimum(s + 1, SEGS - 1)])
    end = jnp.minimum(following, high) - low
    return begin, end


def is_early(device):
    return (device // 8 % 4 + device // 32 <= 1) & (device % 8 < 4)


def move_interior(owns, news, shift):
    shift_row = shift // LANES
    shift_lane = lax.rem(shift, LANES)
    back = lax.rem(LANES - shift_lane, LANES)
    keep = lanes_of(BLOCK) >= shift_lane

    def move(b, carry):
        source = b * BLOCK + shift_row - RIM
        rows = pl.ds(pl.multiple_of(b * BLOCK, BLOCK), BLOCK)
        for own, fresh in zip(owns, news):
            here = own[pl.ds(source, BLOCK), :]
            below = own[pl.ds(source + 1, BLOCK), :]
            fresh[rows, :] = pltpu.roll(jnp.where(keep, here, below), back, 1)
        return carry

    lax.fori_loop(1, BLOCKS, move, 0, unroll=True)


def label_elements(seg_map, seg, low, high):
    first, last = segment_range(seg, low, high)
    element = index_of(BLOCK)

    def segment(s, carry):
        begin, end = segment_span(seg, s, low, high)
        first_block = begin // BLOCK_ELEMS
        last_block = jnp.where(s == last, BLOCKS - 1, (end - 1) // BLOCK_ELEMS)
        rows = pl.ds(pl.multiple_of(first_block * BLOCK, BLOCK), BLOCK)
        seg_map[rows, :] = jnp.where(element + first_block * BLOCK_ELEMS >= begin, s, seg_map[rows, :])

        def fill(b, inner):
            seg_map[pl.ds(pl.multiple_of(b * BLOCK, BLOCK), BLOCK), :] = jnp.full((BLOCK, LANES), s, jnp.int32)
            return inner

        lax.fori_loop(first_block + 1, last_block + 1, fill, 0)
        return carry

    lax.fori_loop(first, last + 1, segment, 0)


def fold(x):
    return x[0:8] + x[8:16] + x[16:24] + x[24:32]


def prepare(w_hbm, m_hbm, v_hbm, g_hbm, old_hbm, new_hbm, seg_hbm,
            pay, w_own, m_own, v_own, u_own, send_core, send_next, w_new, m_new, v_new, u_new, seg_map, info,
            m_in, v_in, g_in, weight_sums, update_sums, old, new, seg, sems, scalar_sems):
    scalar_copies = [
        pltpu.make_async_copy(old_hbm, old, scalar_sems.at[0]),
        pltpu.make_async_copy(seg_hbm, seg, scalar_sems.at[1]),
        pltpu.make_async_copy(new_hbm, new, scalar_sems.at[2]),
    ]
    for copy in scalar_copies:
        copy.start()
    pieces = []
    for p, (begin, end) in enumerate(PIECES):
        rows = pl.ds(begin * BLOCK, (end - begin) * BLOCK)
        pieces.append([
            pltpu.make_async_copy(source.at[rows], target.at[rows], sems.at[p, a])
            for a, (source, target) in enumerate(((g_hbm, g_in), (v_hbm, v_in), (m_hbm, m_in), (w_hbm, w_own)))
        ])
        for copy in pieces[-1]:
            copy.start()
    device = lax.axis_index("dp")
    even = lax.rem(device, 2) == 0
    for copy in scalar_copies:
        copy.wait()
    low = old[device]
    high = old[device + 1]
    count = high - low
    new_low = new[device]
    new_high = new[device + 1]
    row = lax.broadcasted_iota(jnp.int32, (8, LANES), 0)
    facts = jnp.where(row == 0, new_low - low + MARGIN, new_low)
    facts = jnp.where(row == 1, high - new_low, facts)
    info[...] = jnp.where(row == 2, new_high - new_low, facts)
    first, last = segment_range(seg, low, high)

    def update(b, carry):
        rows = pl.ds(pl.multiple_of(b * BLOCK, BLOCK), BLOCK)
        grad = g_in[rows, :].astype(jnp.float32)
        weight = w_own[rows, :]
        moment = BETA_ONE * m_in[rows, :] + (1.0 - BETA_ONE) * grad
        second = BETA_TWO * v_in[rows, :] + (1.0 - BETA_TWO) * grad * grad
        step = moment * (1.0 / CORR_ONE) / (jnp.sqrt(second * (1.0 / CORR_TWO)) + EPSILON) + DECAY * weight
        m_own[rows, :] = moment
        v_own[rows, :] = second
        u_own[rows, :] = step
        short = pl.ds(pl.multiple_of(b * 8, 8), 8)
        weight_sum = fold(weight * weight)
        update_sum = fold(step * step)
        weight_sums[short, :] = weight_sum
        update_sums[short, :] = update_sum
        return carry[0] + weight_sum, carry[1] + update_sum

    zero = jnp.zeros((8, LANES), jnp.float32)
    live_sums = (zero, zero)
    for (begin, end), copies in zip(PIECES, pieces):
        for copy in copies:
            copy.wait()
        live_sums = lax.fori_loop(begin, min(end, LIVE), update, live_sums, unroll=True)
        lax.fori_loop(min(end, LIVE), end, update, (zero, zero), unroll=True)

    cut = count - MARGIN
    cut_row = cut // LANES
    cut_lane = lax.rem(cut, LANES)
    back = lax.rem(LANES - cut_lane, LANES)
    for a, source in enumerate((w_own, m_own, v_own, u_own)):
        here = source[pl.ds(cut_row, RIM), :]
        below = source[pl.ds(cut_row + 1, RIM), :]
        tail = pltpu.roll(jnp.where(lanes_of(RIM) >= cut_lane, here, below), back, 1)
        head = source[pl.ds(0, RIM), :]
        send_next[a] = jnp.where(even, head, tail)
        send_core[a] = jnp.where(even, tail, head)

    element = index_of(BLOCK)

    lane = lanes_of(8)

    def masked(b, sums, begin, end):
        weight_sum, update_sum = sums
        rows = pl.ds(pl.multiple_of(b * BLOCK, BLOCK), BLOCK)
        place = element + b * BLOCK_ELEMS
        inside = (place >= begin) & (place < end)
        weight = w_own[rows, :]
        step = u_own[rows, :]
        weight_sum = weight_sum + fold(jnp.where(inside, weight * weight, 0.0))
        update_sum = update_sum + fold(jnp.where(inside, step * step, 0.0))
        return weight_sum, update_sum

    def pack(s, weight_sum, update_sum):
        weight_sum = jnp.sum(jnp.sum(weight_sum, axis=0, keepdims=True), axis=1, keepdims=True)
        update_sum = jnp.sum(jnp.sum(update_sum, axis=0, keepdims=True), axis=1, keepdims=True)
        return jnp.where(lane == s, weight_sum, 0.0) + jnp.where(lane == SEGS + s, update_sum, 0.0)

    def segment(s, packed):
        begin, end = segment_span(seg, s, low, high)
        first_block = begin // BLOCK_ELEMS
        last_block = (end - 1) // BLOCK_ELEMS

        def edge(b, sums):
            return masked(b, sums, begin, end)

        def whole(group, sums):
            weight_sum, update_sum = sums
            for b in range(8):
                block = group * 8 + b
                inner = (block > first_block) & (block < last_block)
                short = pl.ds(pl.multiple_of(group * 64 + b * 8, 8), 8)
                weight_sum = weight_sum + jnp.where(inner, weight_sums[short, :], 0.0)
                update_sum = update_sum + jnp.where(inner, update_sums[short, :], 0.0)
            return weight_sum, update_sum

        sums = edge(first_block, (zero, zero))
        sums = lax.fori_loop((first_block + 1) // 8, (last_block + 7) // 8, whole, sums)
        sums = lax.fori_loop(jnp.maximum(last_block, first_block + 1), last_block + 1, edge, sums)
        return packed + pack(s, *sums)

    def one_tensor():
        sums = live_sums
        for b in range(LIVE, BLOCKS):
            sums = masked(b, sums, 0, count)
        return pack(first, *sums)

    def several_tensors():
        return lax.fori_loop(first, last + 1, segment, jnp.zeros((8, LANES), jnp.float32))

    packed = lax.cond(first == last, one_tensor, several_tensors)
    for row in range(0, N_DP, 8):
        pay[pl.ds(row, 8), :] = packed

    @pl.when(is_early(device))
    def _():
        move_interior((w_own, m_own, v_own, u_own), (w_new, m_new, v_new, u_new), new_low - low + MARGIN)
        label_elements(seg_map, seg, new_low, new_high)


def finish(parts, w_own, m_own, v_own, u_own, from_next, from_core, w_pre, m_pre, v_pre, u_pre, seg_pre,
           info, seg_hbm, w_out, m_out, v_out,
           w_late, m_late, v_late, u_late, seg_late, w_new, heads, tails, rims, seg, sems, seg_sem):
    device = lax.axis_index("dp")
    facts = info[...]
    shift = facts[0, 0]
    cut = facts[1, 0]
    count = facts[2, 0]
    low = facts[3, 0]
    early = is_early(device)
    owns = (w_own, m_own, v_own, u_own)
    outs = (w_out, m_out, v_out)
    body = pl.ds(RIM, TAIL - RIM)

    def emit(news, seg_map):
        body_copies = [pltpu.make_async_copy(news[a].at[body], outs[a].at[body], sems.at[a]) for a in (1, 2)]
        for copy in body_copies:
            copy.start()
        sums = jnp.broadcast_to(jnp.sum(parts[...], axis=0, keepdims=True), (8, LANES))
        roots = jnp.sqrt(sums)
        rates = LEARN * roots / (pltpu.roll(roots, SEGS, 1) + EPSILON)

        def rate_of(labels):
            pieces = [jnp.take_along_axis(rates, labels[r:r + 8], axis=1) for r in range(0, labels.shape[0], 8)]
            return jnp.concatenate(pieces, axis=0)

        def apply(b, carry):
            rows = pl.ds(pl.multiple_of(b * BLOCK, BLOCK), BLOCK)
            w_new[rows, :] = news[0][rows, :] - rate_of(seg_map[rows, :]) * news[3][rows, :]
            return carry

        for p, (begin, end) in enumerate(BODY_PIECES):
            lax.fori_loop(begin, end, apply, 0, unroll=True)
            rows = pl.ds(begin * BLOCK, (end - begin) * BLOCK)
            body_copies.append(pltpu.make_async_copy(w_new.at[rows], w_out.at[rows], sems.at[9 + p]))
            body_copies[-1].start()
        shift_row = shift // LANES
        shift_lane = lax.rem(shift, LANES)
        back = lax.rem(LANES - shift_lane, LANES)
        even = lax.rem(device, 2) == 0

        for a in range(4):
            heads[a, pl.ds(0, RIM), :] = jnp.where(even, from_next[a], from_core[a])
            rims[a, pl.ds(8, RIM), :] = jnp.where(even, from_core[a], from_next[a])

        keep = lanes_of(RIM) >= shift_lane
        tail_live = index_of(TAIL_ROWS) + TAIL * LANES < count
        for a in range(4):
            heads[a, pl.ds(RIM, 72), :] = owns[a][pl.ds(0, 72), :]
            here = heads[a, pl.ds(shift_row, RIM), :]
            below = heads[a, pl.ds(shift_row + 1, RIM), :]
            heads[a, pl.ds(104, RIM), :] = pltpu.roll(jnp.where(keep, here, below), back, 1)
            tails[a, pl.ds(0, TAIL_ROWS), :] = jnp.where(tail_live, news[a][pl.ds(TAIL, TAIL_ROWS), :], 0.0)

        cut_row = jnp.minimum(cut // LANES - TAIL, TAIL_ROWS)
        cut_lane = lax.rem(cut, LANES)
        place = index_of(40) + (cut_row + TAIL) * LANES
        taken = (place >= cut) & (place < count)
        fits = lanes_of(40) < LANES - cut_lane
        rows = pl.ds(cut_row, 40)
        for a in range(4):
            here = rims[a, pl.ds(8, 40), :]
            above = rims[a, pl.ds(7, 40), :]
            incoming = pltpu.roll(jnp.where(fits, here, above), cut_lane, 1)
            tails[a, rows, :] = jnp.where(taken, incoming, tails[a, rows, :])

        top = pl.ds(104, RIM)
        heads[0, top, :] = heads[0, top, :] - rate_of(seg_map[pl.ds(0, RIM), :]) * heads[3, top, :]
        bottom = pl.ds(0, TAIL_ROWS)
        tails[0, bottom, :] = tails[0, bottom, :] - rate_of(seg_map[pl.ds(TAIL, TAIL_ROWS), :]) * tails[3, bottom, :]
        edge_copies = []
        for a in range(3):
            edge_copies.append(pltpu.make_async_copy(heads.at[a, top], outs[a].at[pl.ds(0, RIM)], sems.at[3 + a]))
            edge_copies.append(
                pltpu.make_async_copy(tails.at[a, bottom], outs[a].at[pl.ds(TAIL, TAIL_ROWS)], sems.at[6 + a]))
        for copy in edge_copies:
            copy.start()

        for copy in body_copies + edge_copies:
            copy.wait()

    @pl.when(early)
    def _():
        emit((w_pre, m_pre, v_pre, u_pre), seg_pre)

    @pl.when(jnp.logical_not(early))
    def _():
        copy = pltpu.make_async_copy(seg_hbm, seg, seg_sem)
        copy.start()
        news = (w_late, m_late, v_late, u_late)
        move_interior(owns, news, shift)
        copy.wait()
        label_elements(seg_late, seg, low, low + count)
        emit(news, seg_late)


def in_hbm(*arrays):
    return [pltpu.with_memory_space_constraint(x, pltpu.HBM) for x in arrays]


def shards(params, first_moment, second_moment, grads, old_bounds, new_bounds, seg_start):
    hbm = pl.BlockSpec(memory_space=pltpu.HBM)
    vmem = pl.BlockSpec(memory_space=pltpu.VMEM)
    bounds = pltpu.SMEM((N_DP + 1,), jnp.int32)
    starts = pltpu.SMEM((SEGS,), jnp.int32)
    block_sums = pltpu.VMEM((32 * 8, LANES), jnp.float32)
    f32 = jnp.float32
    own = jax.ShapeDtypeStruct((PAD_ROWS, LANES), f32)
    rim = jax.ShapeDtypeStruct((4, RIM, LANES), f32)
    state = pltpu.VMEM((ROWS, LANES), f32)
    flat = [x.reshape(ROWS, LANES) for x in (params, first_moment, second_moment, grads)]
    moved = jax.ShapeDtypeStruct((ROWS, LANES), f32)
    labels = jax.ShapeDtypeStruct((ROWS, LANES), jnp.int32)
    pay, w_own, m_own, v_own, u_own, send_core, send_next, *early = pl.pallas_call(
        prepare,
        out_shape=(jax.ShapeDtypeStruct((N_DP, LANES), f32), own, own, own, own, rim, rim,
                   moved, moved, moved, moved, labels, jax.ShapeDtypeStruct((8, LANES), jnp.int32)),
        in_specs=[hbm] * 7,
        out_specs=[vmem] * 13,
        scratch_shapes=[state, state, pltpu.VMEM((ROWS, LANES), jnp.bfloat16), block_sums, block_sums,
                        bounds, bounds, starts,
                        pltpu.SemaphoreType.DMA((4, 4)), pltpu.SemaphoreType.DMA((3,))],
        compiler_params=pltpu.CompilerParams(vmem_limit_bytes=24 * 2**20),
    )(*in_hbm(*flat, old_bounds, new_bounds, seg_start))
    pairs = [(i, i ^ 1) for i in range(N_DP)]
    between = [(i, (i + (1 if i % 2 else -1)) % N_DP) for i in range(N_DP)]
    from_next = lax.ppermute(send_next, "dp", between)
    from_core = lax.ppermute(send_core, "dp", pairs)
    parts = lax.all_to_all(pay, "dp", 0, 0, tiled=True)
    outs = pl.pallas_call(
        finish,
        out_shape=(jax.ShapeDtypeStruct((ROWS, LANES), f32),) * 3,
        in_specs=[vmem] * 13 + [hbm],
        out_specs=[hbm] * 3,
        scratch_shapes=[state] * 4 + [pltpu.VMEM((ROWS, LANES), jnp.int32), state]
        + [pltpu.VMEM((4, 136, LANES), f32), pltpu.VMEM((4, 136, LANES), f32), pltpu.VMEM((4, 48, LANES), f32),
           starts, pltpu.SemaphoreType.DMA((13,)), pltpu.SemaphoreType.DMA],
        compiler_params=pltpu.CompilerParams(vmem_limit_bytes=24 * 2**20),
    )(parts, w_own, m_own, v_own, u_own, from_next, from_core, *early, *in_hbm(seg_start))
    return tuple(x.reshape(-1) for x in outs)


def solution(mesh):
    return jax.shard_map(
        shards,
        mesh=mesh,
        in_specs=(P("dp"), P("dp"), P("dp"), P("dp"), P(), P(), P()),
        out_specs=(P("dp"), P("dp"), P("dp")),
        check_vma=False,
    )
```
